32 devices in a mesh: dp: 8 (over z, y), mp: 4 (over x, core).
Axes of the slice: x: 2, y: 2, z: 4, core: 2. Of those that a mesh axis runs over, the one named last changes fastest.
Arguments:
- clean_latent: float32 [16, 768, 20], P('dp', 'mp'), may hold values from -6 to 6
- noise_draw: float32 [16, 768, 20], P('dp', 'mp'), may hold values from -6 to 6
- captions: bfloat16 [16, 256, 768], P('dp'), may hold values from -6 to 6
- caption_len: int32 [16], P('dp'), may hold values from 5 to 256, as said below
- timestep: int32 [16], P('dp'), may hold values from 0 to 999
- step_weight: float32 [1000], replicated, may hold values from 0.25 to 4
- step_count: int32 [1], replicated, may hold values from 2 to 20
- unit_slot: int32 [26], replicated, may hold values from 0 to 39, as said below
- master: float32 [40, 768, 768], P('dp', 'mp'), may hold values from -0.21875 to 0.21875
- first_moment: float32 [40, 768, 768], P('dp', 'mp'), may hold values from -8.34465e-07 to 8.34465e-07
- second_moment: float32 [40, 768, 768], P('dp', 'mp'), may hold values from 2.6031255e-16 to 1.0412502e-15
- latent_master: float32 [2, 20, 768], replicated, may hold values from -0.21875 to 0.21875
- latent_first: float32 [2, 20, 768], replicated, may hold values from -4.7683716e-06 to 4.7683716e-06
- latent_second: float32 [2, 20, 768], replicated, may hold values from 9.300595e-15 to 3.720238e-14
Outputs:
- updated_master: float32 [40, 768, 768], P('dp', 'mp')
- updated_first: float32 [40, 768, 768], P('dp', 'mp')
- updated_second: float32 [40, 768, 768], P('dp', 'mp')
- latent_updated: float32 [2, 20, 768], replicated
- latent_first_out: float32 [2, 20, 768], replicated
- latent_second_out: float32 [2, 20, 768], replicated
- grad_norm: float32 [], replicated
- loss_value: float32 [], replicated
The draws below stay inside these ranges and needn't reach their ends.
Inputs may be any that keep to these rules, and one draw needn't show every extreme that they name: Clip b's caption occupies its first caption_len[b] token slots; some clip uses all 256. All entries differ, so every place holds at most one matrix; matrix u is owned by dp index unit_slot[u] // 5 in its place unit_slot[u] % 5; some dp index owns 5 matrices, every other index owns 0 to 5.
All inputs are finite; a program needn't handle non-finite values.
Results may differ from the reference program's by a relative error of at most 0.017.
Values may be sent and summed in bfloat16 or wider, within the bound.
No kernel may reach another device: no remote copies, remote signals or barrier semaphores. Data moves between devices by JAX's collectives and lax.ppermute only.
A program may use at most 192 MiB of HBM per device.

```python
import math
import jax
import jax.numpy as jnp
from jax import lax

D = 768
H = 12
HD = 64
C = 20
FRAMES = 768
L_TXT = 256
NT = 1000
UNITS = 26
SLOTS = 5
CLIPS = 16
N_DP = 8


def draw_caption_len(key, part):
    key_len, key_pos = jax.random.split(key)
    values = jax.random.randint(key_len, (CLIPS,), 5, L_TXT + 1)
    position = jax.random.randint(key_pos, (), 0, CLIPS)
    return values.at[position].set(L_TXT).astype(jnp.int32)


def draw_unit_slot(key, part):
    subkeys = jax.random.split(key, 3)
    owner = jax.random.randint(subkeys[0], (), 0, N_DP)
    order = jax.random.permutation(subkeys[1], UNITS)
    others = jax.random.permutation(subkeys[2], (N_DP - 1) * SLOTS)[:UNITS - SLOTS]
    others = jnp.where(others >= owner * SLOTS, others + SLOTS, others)
    slot_ids = jnp.concatenate([owner * SLOTS + jnp.arange(SLOTS), others]).astype(jnp.int32)
    return jnp.zeros((UNITS,), jnp.int32).at[order].set(slot_ids)


def set_ends(array, own_key, smallest, high):
    index_at = [jax.random.randint(jax.random.fold_in(own_key, axis), (), 0, length) for axis, length in enumerate(array.shape)]
    widest = array.shape.index(max(array.shape))
    beside = index_at[:widest] + [(index_at[widest] + 1) % array.shape[widest]] + index_at[widest + 1:]
    return array.at[tuple(index_at)].set(smallest).at[tuple(beside)].set(high)


def block_levels(stream_key, extent, shards, least, top_value):
    factor_of, own = 1.0, jax.random.fold_in(stream_key, 6)
    for dim, blocks in shards:
        steps = jnp.exp(jax.random.uniform(jax.random.fold_in(own, dim), (blocks,), jnp.float32, least / len(shards), top_value / len(shards)))
        factor_of = factor_of * jnp.repeat(steps, extent[dim] // blocks).reshape([-1 if axis == dim else 1 for axis in range(len(extent))])
    return factor_of


def centred(key, shape, width, reach, shards=(), held_as=jnp.bfloat16):
    values = jax.random.normal(key, shape, jnp.float32) * width
    if len(shards) > 0:
        values = block_levels(key, shape, shards, -0.22, 0.18) * values
    return jnp.clip(values, min=-reach, max=reach).astype(held_as)


def setup_inputs(seed: int = 0) -> dict:
    arg_keys = jax.random.split(jax.random.key(seed), 15)
    clean_latent = centred(arg_keys[0], (CLIPS, FRAMES, C), 1.0, 6.0, ((0, 8), (1, 4)), jnp.float32)
    noise_draw = centred(arg_keys[1], (CLIPS, FRAMES, C), 1.0, 6.0, ((0, 8), (1, 4)), jnp.float32)
    captions = centred(arg_keys[2], (CLIPS, L_TXT, D), 1.0, 6.0, ((0, 8),))
    caption_len = draw_caption_len(jax.random.fold_in(arg_keys[14], 71), 0)
    timestep = set_ends(jax.random.randint(arg_keys[4], (CLIPS,), 0, NT), jax.random.fold_in(arg_keys[4], 1), 0, NT - 1).astype(jnp.int32)
    step_weight = jnp.clip(jnp.exp(jax.random.uniform(arg_keys[5], (NT,), jnp.float32, math.log(0.25), math.log(4.0))), 0.25, 4.0)
    step_count = jax.random.randint(arg_keys[6], (1,), 2, 21).astype(jnp.int32)
    unit_slot = draw_unit_slot(jax.random.fold_in(arg_keys[14], 71), 0)
    master = centred(arg_keys[8], (N_DP * SLOTS, D, D), D ** -0.5, 0.21875, ((0, 8), (1, 4)), jnp.float32)
    first_moment = centred(arg_keys[9], (N_DP * SLOTS, D, D), (0.11 * 0.002 / (UNITS * D * D + 2 * C * D) ** 0.5), 8.344650268554688e-07, ((0, 8), (1, 4)), jnp.float32)
    second_moment = jnp.clip(jnp.exp(math.log(1.041250190521423e-15) - 1.3862944 * jax.random.uniform(arg_keys[10], (N_DP * SLOTS, D, D), jnp.float32) ** block_levels(arg_keys[10], (N_DP * SLOTS, D, D), ((0, 8), (1, 4)), -0.2, 0.2)), 2.6031254763035573e-16, 1.041250190521423e-15)
    latent_master = centred(arg_keys[11], (2, C, D), D ** -0.5, 0.21875, (), jnp.float32)
    latent_first = centred(arg_keys[12], (2, C, D), (0.11 * 0.002 / (C * D * (UNITS + 2)) ** 0.5), 4.76837158203125e-06, (), jnp.float32)
    latent_second = jnp.clip(jnp.exp(jax.random.uniform(arg_keys[13], (2, C, D), jnp.float32, math.log(9.300595402606405e-15), math.log(3.720238161042562e-14))), 9.300595402606405e-15, 3.720238161042562e-14)
    return dict(clean_latent=clean_latent, noise_draw=noise_draw, captions=captions, caption_len=caption_len, timestep=timestep, step_weight=step_weight, step_count=step_count, unit_slot=unit_slot, master=master, first_moment=first_moment, second_moment=second_moment, latent_master=latent_master, latent_first=latent_first, latent_second=latent_second)


highest = lax.Precision.HIGHEST
beta_first = 0.9
beta_second = 0.999
adam_epsilon = 1e-08
learn_rate = 0.02
decay_rate = 0.1
clip_limit = 0.002
norm_epsilon = 1e-06
masked_score = -1e+30

@jax.custom_vjp
def low(v):
    return lax.optimization_barrier(v.astype(jnp.bfloat16)).astype(jnp.float32)

@jax.custom_vjp
def low_back(v):
    return v

def low_keep(v):
    return (low(v), None)

def low_pass(kept, grad):
    return (grad,)

def back_keep(v):
    return (v, None)

def back_low(kept, grad):
    return (low(grad),)
low.defvjp(low_keep, low_pass)
low_back.defvjp(back_keep, back_low)

def rounded_both(values):
    return low(low_back(values))

def product(form, left, right):
    return jnp.einsum(form, left, right, precision=highest)

def normed(values):
    center = values - lax.optimization_barrier(jnp.mean(values, axis=-1, keepdims=True))
    spread_sq = lax.optimization_barrier(jnp.mean(center * center, axis=-1, keepdims=True))
    return center * lax.rsqrt(spread_sq + norm_epsilon)

def modulate(values, shift, scale):
    return normed(values) * (1.0 + scale[:, None, :]) + shift[:, None, :]

def adamw(weight, moment, square, grad, count):
    moment = beta_first * moment + (1.0 - beta_first) * grad
    square = beta_second * square + (1.0 - beta_second) * grad * grad
    first_fix = 1.0 - jnp.power(beta_first, count)
    second_fix = 1.0 - jnp.power(beta_second, count)
    update = moment / first_fix / (jnp.sqrt(square / second_fix) + adam_epsilon) + decay_rate * weight
    return (weight - learn_rate * update, moment, square)

def sinusoid(timestep):
    half_width = D // 2
    frequency = jnp.exp(-math.log(10000.0) * jnp.arange(half_width).astype(jnp.float32) / half_width)
    angles = timestep.astype(jnp.float32)[:, None] * frequency[None, :]
    return jnp.concatenate([jnp.cos(angles), jnp.sin(angles)], axis=1)

def attend(parts):
    query, keys, values, mask = parts
    scores = low_back(product('fhk,ghk->hfg', query, keys) * HD ** (-0.5))
    scores = jnp.where(mask[None, None, :], scores, masked_score)
    probs = jax.nn.softmax(scores, axis=-1)
    return product('hfg,ghk->fhk', low(probs), values)

def split_heads(values):
    return values.reshape(values.shape[0], values.shape[1], H, HD)

def attention(query, keys, values, mask):
    output = lax.map(jax.checkpoint(attend), (split_heads(query), split_heads(keys), split_heads(values), mask))
    return output.reshape(output.shape[0], output.shape[1], D)

def group_loss(units, latent_weight, batch, total):
    clean, noise, text, lengths, steps_of, weight_clip = batch
    level = (steps_of.astype(jnp.float32) + 0.5) / NT
    noisy = (1.0 - level)[:, None, None] * clean + level[:, None, None] * noise
    target = noise - clean
    cap_mask = jnp.arange(L_TXT)[None, :] < lengths[:, None]
    pooled = lax.optimization_barrier(jnp.sum(text * cap_mask.astype(jnp.float32)[:, :, None], axis=1)) / lengths.astype(jnp.float32)[:, None]
    sinus = low(sinusoid(steps_of))
    cond = low_back(product('bd,de->be', sinus, units[24]) + product('bd,de->be', low(pooled), units[25]))
    modulation = low_back(product('bd,jde->bje', low(jax.nn.silu(cond)), units[16:24]))
    hidden_zero = product('bfc,cd->bfd', noisy, latent_weight[0])
    first_in = low(modulate(hidden_zero, modulation[:, 0], modulation[:, 1]))
    projected = rounded_both(product('bfd,jde->jbfe', first_in, units[0:3]))
    self_mask = jnp.ones((clean.shape[0], FRAMES), bool)
    self_out = rounded_both(attention(projected[0], projected[1], projected[2], self_mask))
    self_branch = low_back(product('bfk,dk->bfd', self_out, units[3]))
    hidden_one = hidden_zero + modulation[:, 2, None, :] * self_branch
    second_in = low(normed(hidden_one))
    cross_query = rounded_both(product('bfd,de->bfe', second_in, units[4]))
    cross_keys = rounded_both(product('bld,de->ble', text, units[5]))
    cross_values = rounded_both(product('bld,de->ble', text, units[6]))
    cross_out = rounded_both(attention(cross_query, cross_keys, cross_values, cap_mask))
    cross_branch = low_back(product('bfk,dk->bfd', cross_out, units[7]))
    hidden_two = hidden_one + cross_branch
    third_in = low(modulate(hidden_two, modulation[:, 3], modulation[:, 4]))
    upper = rounded_both(product('bfd,rde->bfre', third_in, units[8:12]))
    activated = low(jax.nn.gelu(upper, approximate=True))
    mlp_branch = low_back(product('bfrc,rdc->bfd', activated, units[12:16]))
    hidden_three = hidden_two + modulation[:, 5, None, :] * mlp_branch
    final_in = low(modulate(hidden_three, modulation[:, 6], modulation[:, 7]))
    predicted = product('bfd,cd->bfc', final_in, latent_weight[1])
    error = predicted - target
    return jnp.sum(weight_clip[:, None, None] * error * error) / (C * FRAMES * total)

def reference(clean_latent, noise_draw, captions, caption_len, timestep, step_weight, step_count, unit_slot, master, first_moment, second_moment, latent_master, latent_first, latent_second):
    units = low(jnp.swapaxes(master[unit_slot], 1, 2))
    clip_weight = step_weight[timestep]
    total = jnp.sum(clip_weight)
    group = math.gcd(clean_latent.shape[0], 4)
    group_count = clean_latent.shape[0] // group

    def regroup(values):
        return values.reshape((group_count, group) + values.shape[1:])
    batches = tuple((regroup(item) for item in (clean_latent, noise_draw, captions.astype(jnp.float32), caption_len, timestep, clip_weight)))

    def accumulate(running, batch):
        group_value, pullback = jax.vjp(lambda unit_arg, latent_arg: group_loss(unit_arg, latent_arg, batch, total), units, latent_master)
        grad_units, grad_latent = pullback(jnp.ones_like(group_value))
        return ((running[0] + grad_units, running[1] + grad_latent, running[2] + group_value), None)
    start_state = (jnp.zeros_like(units), jnp.zeros_like(latent_master), jnp.zeros((), jnp.float32))
    (grad_units, grad_latent, loss_value), _ = lax.scan(accumulate, start_state, batches)
    square_sum = jnp.sum(grad_units * grad_units) + jnp.sum(grad_latent * grad_latent)
    grad_norm = jnp.sqrt(square_sum)
    factor = clip_limit / jnp.maximum(grad_norm, clip_limit)
    slot_grad = jnp.zeros_like(master).at[unit_slot].set(jnp.swapaxes(grad_units, 1, 2) * factor)
    live_slot = jnp.zeros((master.shape[0],), jnp.float32).at[unit_slot].set(1.0) > 0.5
    count = step_count[0].astype(jnp.float32)
    new_weight, new_moment, new_square = adamw(master, first_moment, second_moment, slot_grad, count)
    keep = live_slot[:, None, None]
    latent_weight, latent_moment, latent_square = adamw(latent_master, latent_first, latent_second, grad_latent * factor, count)
    return (jnp.where(keep, new_weight, master), jnp.where(keep, new_moment, first_moment), jnp.where(keep, new_square, second_moment), latent_weight, latent_moment, latent_square, grad_norm, loss_value)
```

```python
import math

import jax
import jax.numpy as jnp
from jax import lax
from jax.experimental import pallas as pl
from jax.experimental.pallas import tpu as pltpu
from jax.sharding import Mesh
from jax.sharding import PartitionSpec as P

D = 768
HD = 64
C = 20
FRAMES = 768
NT = 1000
UNITS = 26
WIDE = 16

highest = lax.Precision.HIGHEST
beta_first = 0.9
beta_second = 0.999
adam_epsilon = 1e-08
learn_rate = 0.02
decay_rate = 0.1
clip_limit = 0.002
norm_epsilon = 1e-06
masked_score = -1e30
bfloat = jnp.bfloat16
single = jnp.float32


def swap(values, axis, bit=0):
    count = lax.axis_size(axis)
    return lax.ppermute(values, axis, [(i, i ^ (1 << bit)) for i in range(count)])


def dp_bits():
    return lax.axis_size("dp").bit_length() - 1


def step(values, which):
    return swap(values, "mx") if which == "x" else swap(values, "dp", which)


def gather_dp(values):
    values = values[None]
    for bit in range(dp_bits()):
        values = jnp.concatenate([values, swap(values, "dp", bit)], axis=0)
    return values


def flip(values, bit):
    shape = values.shape
    split = values.reshape((shape[0] >> (bit + 1), 2, 1 << bit) + shape[1:])
    return split[:, ::-1].reshape(shape)


def sum_dp(values, relative):
    for bit in range(dp_bits()):
        other = swap(values, "dp", bit)
        values = values + (flip(other, bit) if relative else other)
    return values


def scatter_sum_dp(values):
    for bit in reversed(range(dp_bits())):
        half = values.shape[0] // 2
        values = values[:half] + swap(values[half:], "dp", bit)
    return values[0]


def sum_mp(values):
    values = values + swap(values, "mc")
    return values + swap(values, "mx")


def pair(values, axis, name):
    other = swap(values, name)
    first = lax.axis_index(name) == 0
    return jnp.stack([jnp.where(first, values, other), jnp.where(first, other, values)], axis=axis)


def gather_units(chunk, order):
    pieces = chunk[None]
    for which in order:
        pieces = jnp.concatenate([pieces, step(pieces, which)], axis=0)
    bits = dp_bits()
    tail = chunk.shape
    pieces = pieces.reshape((2,) * (bits + 1) + tail)
    axis_of = {which: bits - i for i, which in enumerate(order)}
    perm = (
        [bits + 1, axis_of["x"], bits + 2]
        + [axis_of[bit] for bit in reversed(range(bits))]
        + [bits + 3, bits + 4]
    )
    return jnp.transpose(pieces, perm).reshape(tail[0], -1, tail[3])


def scatter_units(grads, order):
    bits = dp_bits()
    count, rows, depth = grads.shape
    small = rows // (6 << bits)
    pieces = grads.astype(bfloat).reshape((count, 2, 3) + (2,) * bits + (small, depth))
    axis_of = {bit: 3 + (bits - 1 - bit) for bit in range(bits)}
    axis_of["x"] = 1
    perm = [axis_of[which] for which in reversed(order)] + [0, 2, 3 + bits, 4 + bits]
    pieces = jnp.transpose(pieces, perm)
    for i, which in enumerate(reversed(order)):
        total = pieces[0].astype(single) + step(pieces[1], which).astype(single)
        pieces = total.astype(bfloat) if i < bits else total
    return pieces


def pick_kernel(ids, source, target):
    @pl.loop(0, target.shape[0])
    def _(i):
        target[i] = source[ids[i]]


def pick_blocks(source, ids):
    count = ids.shape[0]
    return pl.pallas_call(
        pick_kernel,
        out_shape=jax.ShapeDtypeStruct((count,) + source.shape[1:], source.dtype),
        grid_spec=pltpu.PrefetchScalarGridSpec(
            num_scalar_prefetch=1,
            grid=(),
            in_specs=[pl.BlockSpec(memory_space=pltpu.VMEM)],
            out_specs=pl.BlockSpec(memory_space=pltpu.VMEM),
        ),
        compiler_params=pltpu.CompilerParams(vmem_limit_bytes=40 << 20),
    )(ids.astype(jnp.int32), source)


def exchange_dp(blocks):
    count = lax.axis_size("dp")
    if count > 8:
        sent = jnp.stack([blocks(k) for k in range(count)])
        index = lax.axis_index("dp")
        ranked = pick_blocks(sent, jnp.arange(count) ^ index)
        got = lax.all_to_all(ranked, "dp", 0, 0, tiled=True)
        return pick_blocks(got, jnp.arange(count) ^ index)
    got = [blocks(0)] * count
    for k in reversed(range(1, count)):
        got[k] = lax.ppermute(blocks(k), "dp", [(i, i ^ k) for i in range(count)])
    return jnp.stack(got)


def normed(values):
    center = values - jnp.mean(values, axis=-1, keepdims=True)
    spread_sq = jnp.mean(center * center, axis=-1, keepdims=True)
    return center * lax.rsqrt(spread_sq + norm_epsilon)


def modulate(values, shift, scale):
    return normed(values) * (1.0 + scale[None, :]) + shift[None, :]


def modulate_back(values, shift, scale, grad):
    _, pullback = jax.vjp(modulate, values, shift, scale)
    return pullback(grad)


def adamw(weight, moment, square, grad, count):
    moment = beta_first * moment + (1.0 - beta_first) * grad
    square = beta_second * square + (1.0 - beta_second) * grad * grad
    first_fix = 1.0 - jnp.power(beta_first, count)
    second_fix = 1.0 - jnp.power(beta_second, count)
    update = (
        moment / first_fix / (jnp.sqrt(square / second_fix) + adam_epsilon) + decay_rate * weight
    )
    return (weight - learn_rate * update, moment, square)


def sinusoid(timestep):
    half_width = D // 2
    frequency = jnp.exp(-math.log(10000.0) * jnp.arange(half_width).astype(single) / half_width)
    angles = timestep.astype(single)[:, None] * frequency[None, :]
    return jnp.concatenate([jnp.cos(angles), jnp.sin(angles)], axis=1)


def matmul(form, left, right):
    return jnp.einsum(form, left, right, preferred_element_type=single)


def masked_scores(query, keys, mask):
    scores = matmul("fhk,ghk->hfg", query, keys) * HD ** (-0.5)
    if mask is None:
        return scores
    return jnp.where(mask[None, None, :], scores, masked_score)


def heads(values):
    return values.reshape(values.shape[0], -1, HD)


def merge(values):
    return values.reshape(values.shape[0], -1)


def attention(query, keys, values, mask):
    scores = masked_scores(heads(query), heads(keys), mask)
    row_max = jnp.max(scores, axis=-1, keepdims=True)
    shifted = jnp.exp(scores - row_max)
    row_total = jnp.sum(shifted, axis=-1, keepdims=True)
    probs = shifted / row_total
    output = matmul("hfg,ghk->fhk", probs.astype(bfloat), heads(values))
    return (merge(output.astype(bfloat)), (row_max + jnp.log(row_total))[..., 0])


def attention_back(query, keys, values, mask, grad_out, log_total):
    query, keys, values, grad_out = (heads(item) for item in (query, keys, values, grad_out))
    probs = jnp.exp(masked_scores(query, keys, mask) - log_total[..., None])
    grad_probs = matmul("fhk,ghk->hfg", grad_out, values)
    inner = jnp.sum(probs * grad_probs, axis=-1, keepdims=True)
    grad_scores = (probs * (grad_probs - inner)).astype(bfloat)
    grad_query = matmul("hfg,ghk->fhk", grad_scores, keys) * HD ** (-0.5)
    grad_keys = matmul("hfg,fhk->ghk", grad_scores, query) * HD ** (-0.5)
    grad_values = matmul("hfg,fhk->ghk", probs.astype(bfloat), grad_out)
    return tuple(merge(item.astype(bfloat)) for item in (grad_query, grad_keys, grad_values))


def spread(values):
    return jnp.concatenate([values, swap(values, "mc")], axis=0)


def collect(left, right):
    own = left.shape[0] // 2
    other = matmul("fk,kd->fd", left[own:], right).astype(bfloat)
    got = swap(other, "mc")
    return matmul("fk,kd->fd", left[:own], right) + got.astype(single)


def body(
    clean_latent,
    noise_draw,
    captions,
    caption_len,
    timestep,
    step_weight,
    step_count,
    unit_slot,
    master,
    first_moment,
    second_moment,
    latent_master,
    latent_first,
    latent_second,
):
    slots = master.shape[0]
    width = master.shape[1]
    n_dp = lax.axis_size("dp")
    index = lax.axis_index("dp")
    column = 2 * lax.axis_index("mx") + lax.axis_index("mc")
    clip = lax.axis_index("mx")
    clips = captions.shape[0]
    owner = unit_slot // slots
    place = unit_slot % slots
    local_ids = index * slots + jnp.arange(slots)
    pick = unit_slot[None, :] == local_ids[:, None]
    live_slot = jnp.any(pick, axis=1)

    master_low = master.astype(bfloat)
    split = master_low.reshape(slots, 3, n_dp, width // (3 * n_dp), D)

    def rows_of(k):
        return lax.dynamic_index_in_dim(split, index ^ k, 2, keepdims=False)

    got = exchange_dp(rows_of)
    got = got.reshape((n_dp * slots,) + got.shape[2:])
    where_at = (owner ^ index) * slots + place
    chunks = pick_blocks(got, where_at[:WIDE])
    z_bits = list(range(1, dp_bits()))
    order_y = z_bits + ["x", 0]
    order_x = z_bits + [0, "x"]
    orders = [order_y, order_x]
    halves = [(0, 1), (2, 3), (4, 5), (6, 7)]
    weights = [None] * WIDE
    for i, group in enumerate(halves):
        whole = gather_units(chunks[group[0] : group[-1] + 1], orders[i % 2])
        for j, u in enumerate(group):
            weights[u] = whole[j]

    far = lax.all_gather(chunks[8:], ("dp", "mx"))
    w_up = far[:, :4].reshape(8 * width, D)
    w_down = far[:, 4:].reshape(8 * width, D)

    table = jnp.arange(step_weight.shape[0])
    clip_weight = jnp.sum(
        jnp.where(timestep[:, None] == table[None, :], step_weight[None, :], 0.0), axis=1
    )
    cap_mask = jnp.arange(captions.shape[1])[None, :] < caption_len[:, None]
    pooled = (
        jnp.sum(jnp.where(cap_mask[:, :, None], captions.astype(single), 0.0), axis=1)
        / caption_len.astype(single)[:, None]
    )
    packed = jnp.concatenate(
        [sinusoid(timestep), pooled, jnp.broadcast_to(clip_weight[:, None], (clips, 128))], axis=1
    )
    packed = gather_dp(packed).reshape(n_dp * clips, -1)
    sinus_low = packed[:, :D].astype(bfloat)
    pooled_low = packed[:, D : 2 * D].astype(bfloat)
    weight_total = jnp.sum(packed[:, 2 * D])

    def held(u):
        return lax.dynamic_index_in_dim(master_low, place[u], 0, keepdims=False)

    zero = jnp.zeros((), bfloat)
    cond_part = matmul(
        "bd,ed->be", jnp.where(owner[24] == index, sinus_low, zero), held(24)
    ) + matmul("bd,ed->be", jnp.where(owner[25] == index, pooled_low, zero), held(25))
    cond_part = sum_dp(cond_part.reshape(n_dp, clips, width), True)
    cond = pair(pair(cond_part, 2, "mc"), 2, "mx").reshape(n_dp * clips, D)
    active = jax.nn.silu(cond).astype(bfloat)
    all_rows = matmul("bd,sed->bse", active, master_low)
    ada = pick[:, 16:24]
    rows = jnp.einsum("sj,bse->bje", ada.astype(single), all_rows, precision=highest)
    rows = scatter_sum_dp(rows.reshape(n_dp, clips, 8, width))
    mine = lax.dynamic_index_in_dim(rows, clip, 0, keepdims=False)
    theirs = swap(lax.dynamic_index_in_dim(rows, 1 - clip, 0, keepdims=False), "mx")
    by_x = jnp.stack(
        [jnp.where(clip == 0, mine, theirs), jnp.where(clip == 0, theirs, mine)], axis=1
    )
    modulation = pair(by_x, 2, "mc").reshape(8, D)

    text = lax.dynamic_index_in_dim(captions, clip, 0, keepdims=False)
    text_mask = lax.dynamic_index_in_dim(cap_mask, clip, 0, keepdims=False)
    my_step = lax.dynamic_index_in_dim(timestep, clip, 0, keepdims=False)
    my_weight = lax.dynamic_index_in_dim(clip_weight, clip, 0, keepdims=False)
    latents = jnp.stack([clean_latent, noise_draw], axis=1)
    away = swap(lax.dynamic_index_in_dim(latents, 1 - clip, 0, keepdims=False), "mx")
    latents = jnp.concatenate(
        [lax.dynamic_index_in_dim(latents, clip, 0, keepdims=False), away], axis=1
    )
    level = (my_step.astype(single) + 0.5) / NT
    noisy = (1.0 - level) * latents[0] + level * latents[1]
    target = latents[1] - latents[0]

    hidden_zero = jnp.einsum("fc,cd->fd", noisy, latent_master[0], precision=highest)
    first_in = spread(modulate(hidden_zero, modulation[0], modulation[1]).astype(bfloat))
    self_query, self_keys, self_values = (
        matmul("fd,ed->fe", first_in, weights[u]).astype(bfloat) for u in range(3)
    )
    self_flat, self_total = attention(self_query, self_keys, self_values, None)
    self_branch = collect(self_flat, weights[3])
    hidden_one = hidden_zero + modulation[2] * self_branch
    second_in = spread(normed(hidden_one).astype(bfloat))
    cross_query = matmul("fd,ed->fe", second_in, weights[4]).astype(bfloat)
    cross_keys = matmul("ld,ed->le", text, weights[5]).astype(bfloat)
    cross_values = matmul("ld,ed->le", text, weights[6]).astype(bfloat)
    cross_flat, cross_total = attention(cross_query, cross_keys, cross_values, text_mask)
    cross_branch = collect(cross_flat, weights[7])
    hidden_two = hidden_one + cross_branch
    third_in = spread(modulate(hidden_two, modulation[3], modulation[4]).astype(bfloat))
    upper = matmul("fd,kd->fk", third_in, w_up).astype(bfloat)
    upper_wide = upper.astype(single)
    activated = jax.nn.gelu(upper_wide, approximate=True).astype(bfloat)
    mlp_branch = collect(activated, w_down)
    hidden_three = hidden_two + modulation[5] * mlp_branch
    final_wide = modulate(hidden_three, modulation[6], modulation[7]).astype(bfloat).astype(single)
    predicted = jnp.einsum("fd,cd->fc", final_wide, latent_master[1], precision=highest)
    error = predicted - target
    loss_local = jnp.sum(my_weight * error * error)

    grad_pred = 2.0 / (C * FRAMES) * my_weight * error / weight_total
    grad_out_proj = jnp.einsum("fc,fd->cd", grad_pred, final_wide, precision=highest)
    grad_final = jnp.einsum("fc,cd->fd", grad_pred, latent_master[1], precision=highest)
    grad_three, shift_f, scale_f = modulate_back(
        hidden_three, modulation[6], modulation[7], grad_final
    )
    gate_m_grad = jnp.sum(grad_three * mlp_branch, axis=0)
    grad_mlp = spread((modulation[5] * grad_three).astype(bfloat))
    grad_act = matmul("fd,kd->fk", grad_mlp, w_down)
    _, gelu_back = jax.vjp(lambda inner_in: jax.nn.gelu(inner_in, approximate=True), upper_wide)
    grad_upper = gelu_back(grad_act)[0].astype(bfloat)
    sums = [None] * WIDE

    def reduce_pairs(first, grads):
        grads = grads.reshape(-1, 2 * width, D)
        for j in range(0, grads.shape[0], 2):
            done = scatter_units(grads[j : j + 2], orders[((first + j) // 2) % 2])
            sums[first + j], sums[first + j + 1] = done[0], done[1]

    grad_far = jnp.concatenate(
        [
            item.astype(bfloat).reshape((2 * n_dp, 4) + chunks.shape[1:])
            for item in (
                matmul("fk,fd->kd", grad_upper, third_in),
                matmul("fk,fd->kd", activated, grad_mlp),
            )
        ],
        axis=1,
    )
    far_sum = lax.psum_scatter(grad_far, ("dp", "mx"), scatter_dimension=0).astype(single)
    for u in range(8):
        sums[8 + u] = far_sum[u]
    grad_third = collect(grad_upper, w_up)
    grad_two, shift_m, scale_m = modulate_back(hidden_two, modulation[3], modulation[4], grad_third)
    grad_two = grad_two + grad_three
    grad_cross = spread(grad_two.astype(bfloat))
    grad_cross_flat = matmul("fd,kd->fk", grad_cross, weights[7]).astype(bfloat)
    grad_w_cross_out = matmul("fk,fd->kd", cross_flat, grad_cross)
    cq_grad, ck_grad, cv_grad = attention_back(
        cross_query, cross_keys, cross_values, text_mask, grad_cross_flat, cross_total
    )
    grad_w_cq = matmul("fk,fd->kd", cq_grad, second_in)
    grad_w_ck = matmul("lk,ld->kd", ck_grad, text)
    grad_w_cv = matmul("lk,ld->kd", cv_grad, text)
    reduce_pairs(4, jnp.concatenate([grad_w_cq, grad_w_ck, grad_w_cv, grad_w_cross_out], axis=0))
    grad_second = collect(cq_grad, weights[4])
    _, norm_back = jax.vjp(normed, hidden_one)
    grad_one = grad_two + norm_back(grad_second)[0]
    gate_a_grad = jnp.sum(grad_one * self_branch, axis=0)
    grad_self = spread((modulation[2] * grad_one).astype(bfloat))
    grad_self_flat = matmul("fd,kd->fk", grad_self, weights[3]).astype(bfloat)
    grad_w_self_out = matmul("fk,fd->kd", self_flat, grad_self)
    sq_grad, sk_grad, sv_grad = attention_back(
        self_query, self_keys, self_values, None, grad_self_flat, self_total
    )
    grad_proj = jnp.concatenate([sq_grad, sk_grad, sv_grad], axis=1)
    grad_w_attn = matmul("fk,fd->kd", grad_proj, first_in)
    reduce_pairs(0, jnp.concatenate([grad_w_attn, grad_w_self_out], axis=0))
    grad_first = collect(grad_proj, jnp.concatenate(weights[0:3], axis=0))
    grad_zero, shift_a, scale_a = modulate_back(
        hidden_zero, modulation[0], modulation[1], grad_first
    )
    grad_zero = grad_zero + grad_one
    grad_in_proj = jnp.einsum("fc,fd->cd", noisy, grad_zero, precision=highest)

    grad_mod = jnp.stack(
        [shift_a, scale_a, gate_a_grad, shift_m, scale_m, gate_m_grad, shift_f, scale_f], axis=0
    )
    grad_mod = (grad_mod + swap(grad_mod, "mc")).astype(bfloat)
    grad_mod = gather_dp(pair(grad_mod, 0, "mx")).reshape(n_dp * clips, 8, D)
    mod_cols = lax.dynamic_index_in_dim(
        grad_mod.reshape(n_dp * clips, 8, D // width, width), column, 2, keepdims=False
    )
    slot_mod = matmul("sj,bje->sbe", ada.astype(bfloat), mod_cols).astype(bfloat)
    grad_active = matmul("sbe,sed->bd", slot_mod, master_low).reshape(n_dp, clips, D)
    grad_active = sum_mp(sum_dp(grad_active, True)).reshape(n_dp * clips, D)
    _, silu_back = jax.vjp(jax.nn.silu, cond)
    grad_cond = silu_back(grad_active)[0].astype(bfloat)
    cond_cols = lax.dynamic_index_in_dim(
        grad_cond.reshape(n_dp * clips, D // width, width), column, 1, keepdims=False
    )
    is_time, is_pool = pick[:, 24], pick[:, 25]
    slot_out = jnp.where((is_time | is_pool)[:, None, None], cond_cols[None], slot_mod)
    slot_in = jnp.where(
        is_time[:, None, None],
        sinus_low[None],
        jnp.where(is_pool[:, None, None], pooled_low[None], active[None]),
    )
    slot_grad = matmul("sbe,sbd->sed", slot_out, slot_in)

    def gram(values):
        return matmul("bd,cd->bc", values, values)

    flat_mod = grad_mod.reshape(n_dp * clips, 8 * D)
    thin_square = jnp.sum(gram(active) * gram(flat_mod)) + jnp.sum(
        (gram(sinus_low) + gram(pooled_low)) * gram(grad_cond)
    )

    reduced = jnp.stack(sums)
    wide_square = jnp.sum(reduced * reduced)
    reduced_low = reduced.astype(bfloat)
    at_slot = jnp.argmax(
        unit_slot[None, :WIDE] == jnp.arange(n_dp * slots)[:, None], axis=1
    ).reshape(n_dp, slots)

    relative = jnp.arange(n_dp) ^ index
    routes = pick_blocks(reduced_low, at_slot[relative].reshape(-1))
    routes = routes.reshape((n_dp, slots) + routes.shape[1:])
    routed = exchange_dp(lambda k: routes[k])
    routed = pick_blocks(routed, relative)
    routed = jnp.transpose(routed, (1, 2, 0, 3, 4)).reshape(slots, width, D).astype(single)
    is_wide = jnp.any(pick[:, :WIDE], axis=1)
    owned = jnp.where(is_wide[:, None, None], routed, slot_grad)

    pad = jnp.zeros((2 * C, 128), single).at[0, 0].set(loss_local)
    small = jnp.concatenate(
        [jnp.concatenate([grad_in_proj, grad_out_proj], axis=0), pad], axis=1
    )
    small = sum_mp(sum_dp(small, False))
    latent_grad = small[:, :D].reshape(2, C, D)
    loss_sum = small[0, D]
    wide_total = sum_mp(sum_dp(jnp.broadcast_to(wide_square, (8, 128)), False))[0, 0]
    square_sum = wide_total + thin_square + jnp.sum(latent_grad * latent_grad)
    grad_norm = jnp.sqrt(square_sum)
    factor = clip_limit / jnp.maximum(grad_norm, clip_limit)
    count = step_count[0].astype(single)
    new_weight, new_moment, new_square = adamw(
        master, first_moment, second_moment, owned * factor, count
    )
    keep = live_slot[:, None, None]
    latent_weight, latent_moment, latent_square = adamw(
        latent_master, latent_first, latent_second, latent_grad * factor, count
    )
    loss_value = loss_sum / (C * FRAMES * weight_total)
    return (
        jnp.where(keep, new_weight, master),
        jnp.where(keep, new_moment, first_moment),
        jnp.where(keep, new_square, second_moment),
        latent_weight,
        latent_moment,
        latent_square,
        grad_norm,
        loss_value,
    )


def solution(mesh):
    n_dp, n_mp = mesh.shape["dp"], mesh.shape["mp"]
    fine = Mesh(mesh.devices.reshape(n_dp, n_mp // 2, 2), ("dp", "mx", "mc"))
    frames = P("dp", ("mx", "mc"), None)
    placed = (
        frames,
        frames,
        P("dp", None, None),
        P("dp"),
        P("dp"),
        P(),
        P(),
        P(),
        frames,
        frames,
        frames,
        P(),
        P(),
        P(),
    )
    return jax.shard_map(
        body,
        mesh=fine,
        in_specs=placed,
        out_specs=(frames, frames, frames, P(), P(), P(), P(), P()),
        check_vma=False,
    )
```

```python
import functools
import math

import jax
import jax.numpy as jnp
from jax import lax
from jax.experimental import pallas as pl
from jax.experimental.pallas import tpu as pltpu
from jax.sharding import Mesh
from jax.sharding import PartitionSpec as P

D = 768
HD = 64
C = 20
FRAMES = 768
NT = 1000
UNITS = 26
WIDE = 16

highest = lax.Precision.HIGHEST
beta_first = 0.9
beta_second = 0.999
adam_epsilon = 1e-08
learn_rate = 0.02
decay_rate = 0.1
clip_limit = 0.002
norm_epsilon = 1e-06
masked_score = -1e30
bfloat = jnp.bfloat16
single = jnp.float32


def swap(values, axis, bit=0):
    count = lax.axis_size(axis)
    return lax.ppermute(values, axis, [(i, i ^ (1 << bit)) for i in range(count)])


def dp_bits():
    return lax.axis_size("dp").bit_length() - 1


def step(values, which):
    return swap(values, "mx") if which == "x" else swap(values, "dp", which)


def gather_dp(values):
    values = values[None]
    for bit in range(dp_bits()):
        values = jnp.concatenate([values, swap(values, "dp", bit)], axis=0)
    return values


def sum_dp(values):
    for bit in range(dp_bits()):
        values = values + swap(values, "dp", bit)
    return values


def sum_mp(values):
    values = values + swap(values, "mc")
    return values + swap(values, "mx")


def pair(values, axis, name):
    other = swap(values, name)
    first = lax.axis_index(name) == 0
    return jnp.stack([jnp.where(first, values, other), jnp.where(first, other, values)], axis=axis)


def tie(*values):
    return lax.optimization_barrier(values)


def high():
    return lax.axis_size("dp") // 2


def shift(values, by):
    count = lax.axis_size("dp")
    return lax.ppermute(values, "dp", [(i, (i + 2 * by) % count) for i in range(count)])


class Gather:
    def __init__(self, chunk=None):
        self.ring, self.pieces, self.done, self.got = [chunk], None, [], None

    def send_ring(self):
        last = len(self.ring) == 3
        for _ in range(high() - 4 if last else 0):
            self.ring.append(shift(self.ring[-1], 1))
        self.got = shift(self.ring[-1], 1)

    def closed(self):
        return len(self.ring) == high()

    def send(self, which):
        self.done.append(which)
        self.got = step(self.pieces, which)

    def take(self, got):
        if self.pieces is not None:
            self.pieces = jnp.stack([self.pieces, got])
            return
        self.ring.append(got)
        if self.closed():
            self.pieces = jnp.stack(self.ring)

    def halves(self):
        units = self.pieces.shape[1] // 2
        parts = tie(self.pieces[:, :units], self.pieces[:, units:])
        both = Gather(), Gather()
        for part, pieces in zip(both, parts):
            part.pieces = pieces
        return both

    def laid(self):
        x, y = (0, 1) if self.done[-1] == "x" else (1, 0)
        pieces = jnp.transpose(self.pieces, [3, x, 4, 2, y, 5, 6])
        return pieces.reshape(pieces.shape[0], -1, D)


class Scatter:
    def __init__(self, pieces):
        self.pieces, self.got, self.steps = pieces, None, 0

    def send(self, which):
        self.got = step(self.pieces[1], which)

    def send_ring(self):
        if self.steps == 2:
            self.sum = self.pieces[1]
        last = self.steps == 4
        for _ in range(high() - 4 if last else 0):
            self.got = shift(self.sum, 1)
            self.add_ring(self.got)
        self.got = shift(self.sum, 1)

    def add_ring(self, got):
        self.steps += 1
        own = self.pieces[(self.steps - 1) % high()]
        self.sum = (own.astype(single) + got.astype(single)).astype(bfloat)

    def take(self, got):
        if self.steps < 2:
            self.steps += 1
            self.pieces = (self.pieces[0].astype(single) + got.astype(single)).astype(bfloat)
        else:
            self.add_ring(got)

    def join(self, other):
        both = Scatter(jnp.concatenate([self.pieces, other.pieces], axis=1))
        both.steps = 2
        return both


def cut_units(grads, x_first):
    count, rows, depth = grads.shape
    pieces = grads.astype(bfloat).reshape(count, 2, 3, high(), 2, -1, depth)
    perm = [1, 4, 3, 0, 2, 5, 6] if x_first else [4, 1, 3, 0, 2, 5, 6]
    return jnp.transpose(pieces, perm)


def cut_far(grads, tail, x_first):
    pieces = grads.astype(bfloat).reshape((2, 2, high(), 4) + tail)
    return pieces if x_first else pieces.swapaxes(0, 1)


def land(anchor, *streams):
    held = tie(anchor, *(stream.got for stream in streams))
    for stream, got in zip(streams, held[1:]):
        stream.take(got)
    return held[0]


WHOLE = pl.BlockSpec(memory_space=pltpu.VMEM)


def pick_kernel(ids, source, *targets):
    first = 0
    for target in targets:

        @pl.loop(0, target.shape[0])
        def _(i, first=first, target=target):
            target[i] = source[ids[first + i]]

        first += target.shape[0]


def pick_blocks(source, ids, counts):
    return pl.pallas_call(
        pick_kernel,
        out_shape=[
            jax.ShapeDtypeStruct((size,) + source.shape[1:], source.dtype) for size in counts
        ],
        grid_spec=pltpu.PrefetchScalarGridSpec(
            num_scalar_prefetch=1,
            grid=(),
            in_specs=[WHOLE],
            out_specs=[WHOLE] * len(counts),
        ),
        compiler_params=pltpu.CompilerParams(vmem_limit_bytes=40 << 20),
    )(ids.astype(jnp.int32), source)


def place_kernel(n_in, sizes, to, *refs):
    first = 0
    for source in refs[:n_in]:

        @pl.loop(0, source.shape[0])
        def _(i, first=first, source=source):
            unit = to[first + i]
            start = 0
            for target, size in zip(refs[n_in:], sizes):

                @pl.when((unit >= start) & (unit < start + size))
                def _(start=start, target=target):
                    target[unit - start] = source[i]

                start += size

        first += source.shape[0]


def place_blocks(sources, to, sizes):
    tail = sources[0].shape[1:]
    return pl.pallas_call(
        functools.partial(place_kernel, len(sources), sizes),
        out_shape=[jax.ShapeDtypeStruct((size,) + tail, sources[0].dtype) for size in sizes],
        grid_spec=pltpu.PrefetchScalarGridSpec(
            num_scalar_prefetch=1,
            grid=(),
            in_specs=[WHOLE] * len(sources),
            out_specs=[WHOLE] * len(sizes),
        ),
        compiler_params=pltpu.CompilerParams(vmem_limit_bytes=40 << 20),
    )(to.astype(jnp.int32), *sources)


def route_kernel(count, slots, ids, source, square, *targets):
    lane = lax.broadcasted_iota(jnp.int32, targets[0].shape[1:], 1)
    rest = square[0:1, 0:1]
    parts = []
    for _ in range(3):
        parts.append(rest.astype(bfloat).astype(single))
        rest = rest - parts[-1]
    told = jnp.where(lane < 128, parts[0], jnp.where(lane < 256, parts[1], parts[2]))
    for k, target in enumerate(targets):
        for s in range(slots):
            for h in range(3):
                target[3 * s + h] = source[ids[k * slots + s], h]
        target[3 * slots] = told.astype(bfloat)


def route_blocks(source, ids, square, count):
    slots = ids.shape[0] // count
    shape = (3 * slots + 1,) + source.shape[2:]
    return pl.pallas_call(
        functools.partial(route_kernel, count, slots),
        out_shape=[jax.ShapeDtypeStruct(shape, source.dtype)] * count,
        grid_spec=pltpu.PrefetchScalarGridSpec(
            num_scalar_prefetch=1,
            grid=(),
            in_specs=[WHOLE, WHOLE],
            out_specs=[WHOLE] * count,
        ),
        compiler_params=pltpu.CompilerParams(vmem_limit_bytes=40 << 20),
    )(ids.astype(jnp.int32), source, square)


def exchange_dp(blocks):
    count = lax.axis_size("dp")
    if count != 8:
        relative = jnp.arange(count) ^ lax.axis_index("dp")
        ranked = pick_blocks(jnp.stack(blocks), relative, (count,))[0]
        got = lax.all_to_all(ranked, "dp", 0, 0, tiled=True)
        got = pick_blocks(got, relative, (count,))[0]
        return [got.reshape((-1,) + got.shape[2:])]
    got = [blocks[0]] * count
    for k in (7, 6, 5, 4, 1, 2, 3):
        got[k] = lax.ppermute(blocks[k], "dp", [(i, i ^ k) for i in range(count)])
    return got


def adamw(weight, moment, square, grad, first_fix, second_fix):
    moment = beta_first * moment + (1.0 - beta_first) * grad
    square = beta_second * square + (1.0 - beta_second) * grad * grad
    update = (moment / first_fix) / (
        jnp.sqrt(square / second_fix) + adam_epsilon
    ) + decay_rate * weight
    return (weight - learn_rate * update, moment, square)


def adam_kernel(n_src, me, kind, scalars, *refs):
    routed, told, refs = refs[:n_src], refs[n_src : 2 * n_src], refs[2 * n_src :]
    slot_out, slot_in, weight, moment, square, latent_grad, *refs = refs
    latents, (new_weight, new_moment, new_square), refs = refs[:3], refs[3:6], refs[6:]
    new_latents, norm_out, grads = refs[:3], refs[3], refs[4]
    per, rows = routed[0].shape[0], routed[0].shape[2]
    squares = []
    for item in told:
        for j in range(per):
            parts = [item[j, 0, 0:1, 128 * i : 128 * i + 1].astype(single) for i in range(3)]
            squares.append(parts[0] + parts[1] + parts[2])
    while len(squares) > 1:
        squares = [squares[i] + squares[i + 1] for i in range(0, len(squares), 2)]
    norm = jnp.sqrt(squares[0] + scalars[0])
    factor = clip_limit / jnp.maximum(norm, clip_limit)

    @pl.when(pl.program_id(0) == 0)
    def _():
        norm_out[...] = jnp.broadcast_to(norm, norm_out.shape)
        held = [item[...] for item in latents]
        fresh = adamw(*held, latent_grad[...] * factor[None], scalars[1], scalars[2])
        for target, item in zip(new_latents, fresh):
            target[...] = item

    for i in range(n_src):
        for j in range(per):
            at = pl.multiple_of(((i * per + j) ^ me[0]) * rows, rows)
            for h in range(3):
                grads[h, pl.ds(at, rows), :] = routed[i][j, h].astype(single)
    sort = kind[pl.program_id(0)]
    for h in range(3):
        thin = lax.dot_general(
            slot_out[0, h], slot_in[0], (((0,), (0,)), ((), ())), preferred_element_type=single
        )
        grad = jnp.where(sort == 1, grads[h], thin) * factor
        w, m, v = weight[0, h], moment[0, h], square[0, h]
        fresh_w, fresh_m, fresh_v = adamw(w, m, v, grad, scalars[1], scalars[2])
        new_weight[0, h] = jnp.where(sort == 0, w, fresh_w)
        new_moment[0, h] = jnp.where(sort == 0, m, fresh_m)
        new_square[0, h] = jnp.where(sort == 0, v, fresh_v)


def adam_places(me, kind, scalars, routed, slot_out, slot_in, held, latent_grad, latents):
    slots, width, depth = held[0].shape
    head = width // 3
    clips = slot_in.shape[1]
    rows = routed[0].shape[1]
    routed = [item.reshape((-1, 3 * slots + 1, rows, depth)) for item in routed]
    per = routed[0].shape[0]
    big = pl.BlockSpec((1, 3, head, depth), lambda s, *_: (s, 0, 0, 0))
    small = pl.BlockSpec(latent_grad.shape, lambda s, *_: (0, 0, 0))
    out = pl.pallas_call(
        functools.partial(adam_kernel, len(routed)),
        out_shape=[jax.ShapeDtypeStruct((slots, 3, head, depth), single)] * 3
        + [jax.ShapeDtypeStruct(item.shape, single) for item in latents]
        + [jax.ShapeDtypeStruct((8, 128), single)],
        grid_spec=pltpu.PrefetchScalarGridSpec(
            num_scalar_prefetch=3,
            grid=(slots,),
            in_specs=[pl.BlockSpec((per, 3, rows, depth), lambda s, *_: (0, s, 0, 0))]
            * len(routed)
            + [pl.BlockSpec((per, 1, rows, depth), lambda s, *_: (0, 3 * slots, 0, 0))]
            * len(routed)
            + [
                pl.BlockSpec((1, 3, clips, head), lambda s, *_: (s, 0, 0, 0)),
                pl.BlockSpec((1, clips, depth), lambda s, *_: (s, 0, 0)),
                big,
                big,
                big,
            ]
            + [small] * 4,
            out_specs=[big] * 3 + [small] * 3 + [pl.BlockSpec((8, 128), lambda s, *_: (0, 0))],
            scratch_shapes=[pltpu.VMEM((3, head, depth), single)],
        ),
        compiler_params=pltpu.CompilerParams(vmem_limit_bytes=40 << 20),
    )(
        me,
        kind,
        scalars,
        *routed,
        *routed,
        slot_out.reshape(slots, clips, 3, head).swapaxes(1, 2),
        slot_in,
        *(item.reshape(slots, 3, head, depth) for item in held),
        latent_grad,
        *latents,
    )
    places = [item.reshape(slots, width, depth) for item in out[:3]]
    return places + list(out[3:6]) + [out[6][0, 0]]


def normed(values):
    center = values - jnp.mean(values, axis=-1, keepdims=True)
    spread_sq = jnp.mean(center * center, axis=-1, keepdims=True)
    return center * lax.rsqrt(spread_sq + norm_epsilon)


def modulate(values, shift, scale):
    return normed(values) * (1.0 + scale[None, :]) + shift[None, :]


def modulate_back(values, shift, scale, grad):
    _, pullback = jax.vjp(modulate, values, shift, scale)
    return pullback(grad)


def sinusoid(timestep):
    half_width = D // 2
    frequency = jnp.exp(-math.log(10000.0) * jnp.arange(half_width).astype(single) / half_width)
    angles = timestep.astype(single)[:, None] * frequency[None, :]
    return jnp.concatenate([jnp.cos(angles), jnp.sin(angles)], axis=1)


def matmul(form, left, right):
    return jnp.einsum(form, left, right, preferred_element_type=single)


NT_DIMS = (((1,), (1,)), ((), ()))
TN_DIMS = (((0,), (0,)), ((), ()))


def dot(left, right, dims=(((1,), (0,)), ((), ()))):
    return lax.dot_general(left, right, dims, preferred_element_type=single)


def scores_of(keys, query, length):
    scores = dot(keys, query, NT_DIMS) * HD ** (-0.5)
    if length is None:
        return scores
    row = lax.broadcasted_iota(jnp.int32, scores.shape, 0)
    return jnp.where(row < length, scores, masked_score)


def attend_kernel(masked, length, query, keys, values, output, totals):
    limit = length[0] if masked else None
    rows = []
    for h in range(2):
        at = slice(h * HD, (h + 1) * HD)
        scores = scores_of(keys[:, at], query[:, at], limit)
        top = jnp.max(scores, axis=0, keepdims=True)
        shifted = jnp.exp(scores - top)
        total = jnp.sum(shifted, axis=0, keepdims=True)
        probs = (shifted * (1.0 / total)).astype(bfloat)
        rows.append(dot(values[:, at], probs, TN_DIMS))
        totals[0, h : h + 1, :] = top + jnp.log(total)
    output[...] = jnp.concatenate(rows, axis=0).T.astype(bfloat)


def attend_back_kernel(masked, length, query, keys, values, grad_out, totals, dq, dk, dv):
    limit = length[0] if masked else None
    query_rows, key_cols, value_cols = [], [], []
    for h in range(2):
        at = slice(h * HD, (h + 1) * HD)
        q, k, v, do = query[:, at], keys[:, at], values[:, at], grad_out[:, at]
        probs = jnp.exp(scores_of(k, q, limit) - totals[0, h : h + 1, :])
        grad_probs = dot(v, do, NT_DIMS)
        inner = jnp.sum(probs * grad_probs, axis=0, keepdims=True)
        grad_scores = (probs * (grad_probs - inner)).astype(bfloat)
        query_rows.append(dot(k, grad_scores, TN_DIMS))
        key_cols.append(dot(grad_scores, q))
        value_cols.append(dot(probs.astype(bfloat), do))
    scale = HD ** (-0.5)
    dq[...] = (jnp.concatenate(query_rows, axis=0).T * scale).astype(bfloat)
    dk[...] = (jnp.concatenate(key_cols, axis=1) * scale).astype(bfloat)
    dv[...] = jnp.concatenate(value_cols, axis=1).astype(bfloat)


def pair_call(kernel, length, ins, outs, flops):
    def spec(shape):
        if len(shape) == 3:
            return pl.BlockSpec((1,) + shape[1:], lambda i, *_: (i, 0, 0))
        return pl.BlockSpec((shape[0], 2 * HD), lambda i, *_: (0, i))

    masked = length is not None
    length = jnp.zeros((1,), jnp.int32) if length is None else length.reshape(1)
    return pl.pallas_call(
        functools.partial(kernel, masked),
        out_shape=outs,
        grid_spec=pltpu.PrefetchScalarGridSpec(
            num_scalar_prefetch=1,
            grid=(ins[0].shape[1] // (2 * HD),),
            in_specs=[spec(item.shape) for item in ins],
            out_specs=[spec(item.shape) for item in outs],
        ),
        compiler_params=pltpu.CompilerParams(vmem_limit_bytes=48 << 20),
        cost_estimate=pl.CostEstimate(
            flops=flops, bytes_accessed=8 << 20, transcendentals=6 * FRAMES * FRAMES
        ),
    )(length, *ins)


def attention(query, keys, values, length):
    shape = query.shape
    outs = [
        jax.ShapeDtypeStruct(shape, bfloat),
        jax.ShapeDtypeStruct((shape[1] // (2 * HD), 2, shape[0]), single),
    ]
    flops = 16 * shape[0] * keys.shape[0] * shape[1]
    return pair_call(attend_kernel, length, (query, keys, values), outs, flops)


def attention_back(query, keys, values, length, grad_out, totals):
    outs = [jax.ShapeDtypeStruct(item.shape, bfloat) for item in (query, keys, values)]
    flops = 40 * query.shape[0] * keys.shape[0] * query.shape[1]
    ins = (query, keys, values, grad_out, totals)
    return pair_call(attend_back_kernel, length, ins, outs, flops)


def spread(values):
    return jnp.concatenate([values, swap(values, "mc")], axis=0)


def collect(left, right):
    own = left.shape[0] // 2
    other = matmul("fk,kd->fd", left[own:], right).astype(bfloat)
    got = swap(other, "mc")
    return matmul("fk,kd->fd", left[:own], right) + got.astype(single)


def body(
    clean_latent,
    noise_draw,
    captions,
    caption_len,
    timestep,
    step_weight,
    step_count,
    unit_slot,
    master,
    first_moment,
    second_moment,
    latent_master,
    latent_first,
    latent_second,
):
    slots = master.shape[0]
    width = master.shape[1]
    n_dp = lax.axis_size("dp")
    index = lax.axis_index("dp")
    column = 2 * lax.axis_index("mx") + lax.axis_index("mc")
    clip = lax.axis_index("mx")
    clips = captions.shape[0]
    owner = unit_slot // slots
    place = unit_slot % slots
    local_ids = index * slots + jnp.arange(slots)
    pick = unit_slot[None, :] == local_ids[:, None]
    live_slot = jnp.any(pick, axis=1)

    table = jnp.arange(step_weight.shape[0])
    clip_weight = jnp.sum(
        jnp.where(timestep[:, None] == table[None, :], step_weight[None, :], 0.0), axis=1
    )
    cap_mask = jnp.arange(captions.shape[1])[None, :] < caption_len[:, None]
    pooled = (
        jnp.sum(jnp.where(cap_mask[:, :, None], captions.astype(single), 0.0), axis=1)
        / caption_len.astype(single)[:, None]
    )
    packed = jnp.concatenate(
        [sinusoid(timestep), pooled, jnp.broadcast_to(clip_weight[:, None], (clips, 128))], axis=1
    )

    master_low = master.astype(bfloat)
    split = master_low.reshape(slots, 3, n_dp, width // (3 * n_dp), D)
    blocks = [
        lax.dynamic_index_in_dim(split, index ^ k, 2, keepdims=False) for k in range(n_dp)
    ]
    got = exchange_dp(blocks)
    unit_of = jnp.sum(
        jnp.where(
            unit_slot[None, :] == jnp.arange(n_dp * slots)[:, None],
            jnp.arange(UNITS)[None, :] + 1,
            0,
        ),
        axis=1,
    ) - 1
    table = jnp.stack(
        [
            unit_of.reshape(n_dp, slots)[jnp.array([d ^ k for k in range(n_dp)])]
            for d in range(n_dp)
        ]
    )
    unit_at = lax.dynamic_index_in_dim(table, index, 0, keepdims=False).reshape(-1)
    chunk_self, chunk_cross, chunk_far = place_blocks(got, unit_at, (4, 4, 8))
    unit_tail = chunk_far.shape[1:]
    chunk_self, packed = tie(chunk_self, packed)
    near, cross, far = Gather(chunk_self), Gather(chunk_cross), Gather(chunk_far)

    near.send_ring()
    packed = packed[None]
    for bit in range(dp_bits()):
        packed = jnp.concatenate([packed, swap(packed, "dp", bit)], axis=0)
        if bit < 3:
            packed = land(packed, near)
            if bit < 2:
                near.send_ring()
    near_a, near_b = near.halves()
    near_a.pieces, near_b.pieces, cross.ring[0] = tie(
        near_a.pieces, near_b.pieces, cross.ring[0]
    )
    near_a.send(0)
    near_b.send("x")
    cross.send_ring()
    packed = packed.reshape(n_dp * clips, -1)
    sinus_low = packed[:, :D].astype(bfloat)
    pooled_low = packed[:, D : 2 * D].astype(bfloat)
    weight_total = jnp.sum(packed[:, 2 * D])

    def held(u):
        return lax.dynamic_index_in_dim(master_low, place[u], 0, keepdims=False)

    zero = jnp.zeros((), bfloat)
    cond_part = matmul(
        "bd,ed->be", jnp.where(owner[24] == index, sinus_low, zero), held(24)
    ) + matmul("bd,ed->be", jnp.where(owner[25] == index, pooled_low, zero), held(25))
    row = jnp.arange(n_dp * clips)
    reorder = (row[:, None] ^ (index * clips)) == row[None, :]
    reorder = reorder.astype(single)

    def reordered(values):
        return jnp.einsum("bc,cd->bd", reorder, values, precision=highest)

    cond_part = reordered(cond_part)
    cond_part = cond_part + swap(cond_part, "dp", 0)
    for bit in range(1, dp_bits()):
        cond_part = cond_part + swap(cond_part, "dp", bit)
        if bit == 1:
            cond_part = land(cond_part, near_a, near_b, cross)
            near_a.send("x")
            near_b.send(0)
            cross.send_ring()
    cond_part = land(cond_part, cross)
    cross.send_ring()
    cond = pair(pair(cond_part, 1, "mc"), 1, "mx").reshape(n_dp * clips, D)
    cond = tie(reordered(cond))[0]
    active = jax.nn.silu(cond).astype(bfloat)
    all_rows = matmul("bd,sed->bse", active, master_low)
    ada = pick[:, 16:24]
    rows = jnp.einsum("sj,bse->bje", ada.astype(single), all_rows, precision=highest)
    rows = rows.reshape(n_dp, clips, 8, width)
    rows = land(rows, near_a, near_b, cross)
    cross_a, cross_b = cross.halves()
    cross_a.pieces, cross_b.pieces, far.ring[0] = tie(
        cross_a.pieces, cross_b.pieces, far.ring[0]
    )
    cross_a.send(0)
    cross_b.send("x")
    far.send_ring()
    for bit in reversed(range(dp_bits())):
        half = rows.shape[0] // 2
        rows = rows[:half] + swap(rows[half:], "dp", bit)
        if bit == 2:
            rows = land(rows, far)
            far.send_ring()
        if bit == 0:
            rows = land(rows, far, cross_a, cross_b)
            cross_a.send("x")
            cross_b.send(0)
            far.send_ring()
    rows = rows[0]
    mine = lax.dynamic_index_in_dim(rows, clip, 0, keepdims=False)
    theirs = swap(lax.dynamic_index_in_dim(rows, 1 - clip, 0, keepdims=False), "mx")
    by_x = jnp.stack(
        [jnp.where(clip == 0, mine, theirs), jnp.where(clip == 0, theirs, mine)], axis=1
    )
    modulation = tie(pair(by_x, 2, "mc").reshape(8, D))[0]

    text = lax.dynamic_index_in_dim(captions, clip, 0, keepdims=False)
    text_len = lax.dynamic_index_in_dim(caption_len, clip, 0, keepdims=False)
    my_step = lax.dynamic_index_in_dim(timestep, clip, 0, keepdims=False)
    my_weight = lax.dynamic_index_in_dim(clip_weight, clip, 0, keepdims=False)
    latents = jnp.stack([clean_latent, noise_draw], axis=1)
    away = swap(lax.dynamic_index_in_dim(latents, 1 - clip, 0, keepdims=False), "mx")
    latents = jnp.concatenate(
        [lax.dynamic_index_in_dim(latents, clip, 0, keepdims=False), away], axis=1
    )
    level = (my_step.astype(single) + 0.5) / NT
    noisy = (1.0 - level) * latents[0] + level * latents[1]
    target = latents[1] - latents[0]

    hidden_zero = jnp.einsum("fc,cd->fd", noisy, latent_master[0], precision=highest)
    first_in = spread(modulate(hidden_zero, modulation[0], modulation[1]).astype(bfloat))
    w_self = jnp.concatenate([near_a.laid(), near_b.laid()], axis=0)
    first_in = land(first_in, far)
    up, down = far.halves()
    up.send(0)
    down.send("x")
    self_query, self_keys, self_values = (
        matmul("fd,ed->fe", first_in, w_self[u]).astype(bfloat) for u in range(3)
    )
    self_query = land(self_query, cross_a, cross_b)
    self_flat, self_total = attention(self_query, self_keys, self_values, None)
    self_flat = land(self_flat, up, down)
    up.send("x")
    down.send(0)
    w_cross = jnp.concatenate([cross_a.laid(), cross_b.laid()], axis=0)
    weights = [w_self[i] for i in range(4)] + [w_cross[i] for i in range(4)]
    self_branch = collect(self_flat, weights[3])
    hidden_one = hidden_zero + modulation[2] * self_branch
    second_in = spread(normed(hidden_one).astype(bfloat))
    cross_query = matmul("fd,ed->fe", second_in, weights[4]).astype(bfloat)
    cross_keys = matmul("ld,ed->le", text, weights[5]).astype(bfloat)
    cross_values = matmul("ld,ed->le", text, weights[6]).astype(bfloat)
    cross_flat, cross_total = attention(cross_query, cross_keys, cross_values, text_len)
    cross_branch = collect(cross_flat, weights[7])
    hidden_two = hidden_one + cross_branch
    third_in = spread(modulate(hidden_two, modulation[3], modulation[4]).astype(bfloat))
    third_in = land(third_in, up)
    w_up = up.pieces.reshape(-1, D)
    upper = matmul("fd,kd->fk", third_in, w_up).astype(bfloat)
    upper_wide = upper.astype(single)
    activated = jax.nn.gelu(upper_wide, approximate=True).astype(bfloat)
    activated, got = tie(activated, down.got)
    w_down = jnp.stack([down.pieces, got], axis=1).reshape(-1, D)
    mlp_branch = collect(activated, w_down)
    hidden_three = hidden_two + modulation[5] * mlp_branch
    final_wide = modulate(hidden_three, modulation[6], modulation[7]).astype(bfloat).astype(single)
    predicted = jnp.einsum("fd,cd->fc", final_wide, latent_master[1], precision=highest)
    error = predicted - target
    loss_local = jnp.sum(my_weight * error * error)

    grad_pred = 2.0 / (C * FRAMES) * my_weight * error / weight_total
    grad_out_proj = jnp.einsum("fc,fd->cd", grad_pred, final_wide, precision=highest)
    grad_final = jnp.einsum("fc,cd->fd", grad_pred, latent_master[1], precision=highest)
    grad_three, shift_f, scale_f = modulate_back(
        hidden_three, modulation[6], modulation[7], grad_final
    )
    gate_m_grad = jnp.sum(grad_three * mlp_branch, axis=0)
    grad_mlp = spread((modulation[5] * grad_three).astype(bfloat))
    grad_w_down = matmul("fk,fd->kd", activated, grad_mlp)
    down = Scatter(cut_far(grad_w_down, unit_tail, True))
    grad_mlp, down.pieces = tie(grad_mlp, down.pieces)
    down.send("x")
    grad_act = matmul("fd,kd->fk", grad_mlp, w_down)
    _, gelu_back = jax.vjp(lambda inner_in: jax.nn.gelu(inner_in, approximate=True), upper_wide)
    grad_upper = gelu_back(grad_act)[0].astype(bfloat)
    grad_w_up = matmul("fk,fd->kd", grad_upper, third_in)
    up = Scatter(cut_far(grad_w_up, unit_tail, False))
    up.send(0)
    grad_third = collect(grad_upper, w_up)
    grad_two, shift_m, scale_m = modulate_back(hidden_two, modulation[3], modulation[4], grad_third)
    grad_two = grad_two + grad_three
    grad_cross = spread(grad_two.astype(bfloat))
    grad_cross_flat = matmul("fd,kd->fk", grad_cross, weights[7]).astype(bfloat)
    grad_w_cross_out = matmul("fk,fd->kd", cross_flat, grad_cross)
    cq_grad, ck_grad, cv_grad = attention_back(
        cross_query, cross_keys, cross_values, text_len, grad_cross_flat, cross_total
    )
    cq_grad = land(cq_grad, down, up)
    down.send(0)
    up.send("x")
    grad_w_cq = matmul("fk,fd->kd", cq_grad, second_in)
    grad_w_ck = matmul("lk,ld->kd", ck_grad, text)
    grad_w_cv = matmul("lk,ld->kd", cv_grad, text)
    cross_a = Scatter(cut_units(jnp.stack([grad_w_cq, grad_w_ck]), True))
    cross_b = Scatter(cut_units(jnp.stack([grad_w_cv, grad_w_cross_out]), False))
    cross_a.send("x")
    cross_b.send(0)
    grad_second = collect(cq_grad, weights[4])
    _, norm_back = jax.vjp(normed, hidden_one)
    grad_one = grad_two + norm_back(grad_second)[0]
    gate_a_grad = jnp.sum(grad_one * self_branch, axis=0)
    grad_self = spread((modulation[2] * grad_one).astype(bfloat))
    grad_self_flat = matmul("fd,kd->fk", grad_self, weights[3]).astype(bfloat)
    grad_self_flat = land(grad_self_flat, down, up)
    far = up.join(down)
    far.send_ring()
    grad_w_self_out = matmul("fk,fd->kd", self_flat, grad_self)
    self_grads = attention_back(
        self_query, self_keys, self_values, None, grad_self_flat, self_total
    )
    self_grads = jnp.concatenate(self_grads, axis=1)
    self_grads = land(self_grads, cross_a, cross_b, far)
    far.send_ring()
    cross_a.send(0)
    cross_b.send("x")
    grad_w_attn = matmul("fk,fd->kd", self_grads, first_in)
    grad_w_attn = land(grad_w_attn, far)
    far.send_ring()
    near_a = Scatter(cut_units(grad_w_attn[: 4 * width].reshape(2, 2 * width, D), True))
    near_b = Scatter(cut_units(jnp.stack([grad_w_attn[4 * width :], grad_w_self_out]), False))
    near_a.send("x")
    near_b.send(0)
    grad_first = collect(self_grads, jnp.concatenate(weights[0:3], axis=0))
    grad_first = land(grad_first, cross_a, cross_b)
    cross = cross_a.join(cross_b)
    cross.send_ring()
    grad_zero, shift_a, scale_a = modulate_back(
        hidden_zero, modulation[0], modulation[1], grad_first
    )
    grad_zero = land(grad_zero, near_a, near_b, cross, far)
    cross.send_ring()
    near_a.send(0)
    near_b.send("x")
    grad_zero = grad_zero + grad_one
    grad_in_proj = jnp.einsum("fc,fd->cd", noisy, grad_zero, precision=highest)

    grad_mod = jnp.stack(
        [shift_a, scale_a, gate_a_grad, shift_m, scale_m, gate_m_grad, shift_f, scale_f], axis=0
    )
    grad_mod = (grad_mod + swap(grad_mod, "mc")).astype(bfloat)
    for i, bit in enumerate(reversed(range(1, dp_bits()))):
        grad_mod = jnp.stack([grad_mod, swap(grad_mod, "dp", bit)], axis=i)
    grad_mod = land(grad_mod, near_a, near_b, cross)
    near = near_a.join(near_b).pieces
    z_got = [shift(near[j], -j) for j in range(1, high())]
    cross.send_ring()
    grad_mod = pair(grad_mod, dp_bits() - 1, "mx")
    grad_mod = jnp.stack([grad_mod, swap(grad_mod, "dp", 0)], axis=dp_bits() - 1)
    grad_mod = tie(grad_mod.reshape(n_dp * clips, 8, D))[0]
    mod_cols = lax.dynamic_index_in_dim(
        grad_mod.reshape(n_dp * clips, 8, D // width, width), column, 2, keepdims=False
    )
    slot_mod = matmul("sj,bje->sbe", ada.astype(bfloat), mod_cols).astype(bfloat)
    grad_active = matmul("sbe,sed->bd", slot_mod, master_low)
    small = jnp.concatenate([grad_in_proj, grad_out_proj], axis=0)
    pad = jnp.full((2 * C, 128), loss_local, single)
    mixed = jnp.concatenate(
        [
            jnp.pad(reordered(grad_active), ((0, 0), (0, 128))),
            jnp.concatenate([small, pad], axis=1),
        ],
        axis=0,
    )
    mixed = sum_dp(sum_mp(mixed))
    grad_active, small = reordered(mixed[: n_dp * clips, :D]), mixed[n_dp * clips :]
    latent_grad = small[:, :D].reshape(2, C, D)
    loss_sum = small[0, D]

    total = near[0].astype(single)
    for item in z_got:
        total = total + item.astype(single)
    cross.take(cross.got)
    reduced = [total] + [item.sum.astype(single) for item in (cross, far)]
    reduced = jnp.concatenate(reduced, axis=0)
    wide_square = sum_mp(jnp.broadcast_to(jnp.sum(reduced * reduced), (8, 128)))
    wide_at = jnp.where((unit_at >= 0) & (unit_at < WIDE), unit_at, 0)
    routes = route_blocks(reduced.astype(bfloat), wide_at, wide_square, n_dp)
    routed = exchange_dp(routes)
    _, silu_back = jax.vjp(jax.nn.silu, cond)
    grad_cond = silu_back(grad_active)[0].astype(bfloat)
    cond_cols = lax.dynamic_index_in_dim(
        grad_cond.reshape(n_dp * clips, D // width, width), column, 1, keepdims=False
    )
    is_time, is_pool = pick[:, 24], pick[:, 25]
    slot_out = jnp.where((is_time | is_pool)[:, None, None], cond_cols[None], slot_mod)
    slot_in = jnp.where(
        is_time[:, None, None],
        sinus_low[None],
        jnp.where(is_pool[:, None, None], pooled_low[None], active[None]),
    )
    def gram(values):
        return matmul("bd,cd->bc", values, values)

    flat_mod = grad_mod.reshape(n_dp * clips, 8 * D)
    thin_square = jnp.sum(gram(active) * gram(flat_mod)) + jnp.sum(
        (gram(sinus_low) + gram(pooled_low)) * gram(grad_cond)
    )

    rest_square = thin_square + jnp.sum(latent_grad * latent_grad)
    count = step_count[0].astype(single)
    is_wide = jnp.any(pick[:, :WIDE], axis=1)
    kind = jnp.where(is_wide, 1, jnp.where(live_slot, 2, 0)).astype(jnp.int32)
    fixes = [1.0 - jnp.power(beta_first, count), 1.0 - jnp.power(beta_second, count)]
    *outputs, grad_norm = adam_places(
        index.reshape(1).astype(jnp.int32),
        kind,
        jnp.stack([rest_square] + fixes),
        routed,
        slot_out,
        slot_in,
        (master, first_moment, second_moment),
        latent_grad,
        (latent_master, latent_first, latent_second),
    )
    loss_value = loss_sum / (C * FRAMES * weight_total)
    return (*outputs, grad_norm, loss_value)


def solution(mesh):
    n_dp, n_mp = mesh.shape["dp"], mesh.shape["mp"]
    fine = Mesh(mesh.devices.reshape(n_dp, n_mp // 2, 2), ("dp", "mx", "mc"))
    frames = P("dp", ("mx", "mc"), None)
    placed = (
        frames,
        frames,
        P("dp", None, None),
        P("dp"),
        P("dp"),
        P(),
        P(),
        P(),
        frames,
        frames,
        frames,
        P(),
        P(),
        P(),
    )
    return jax.shard_map(
        body,
        mesh=fine,
        in_specs=placed,
        out_specs=(frames, frames, frames, P(), P(), P(), P(), P()),
        check_vma=False,
    )
```

```python
import functools
import math

import jax
import jax.numpy as jnp
from jax import lax
from jax.experimental import pallas as pl
from jax.experimental.pallas import tpu as pltpu
from jax.sharding import Mesh
from jax.sharding import PartitionSpec as P

D = 768
HD = 64
C = 20
FRAMES = 768
NT = 1000
UNITS = 26
WIDE = 16

highest = lax.Precision.HIGHEST
beta_first = 0.9
beta_second = 0.999
adam_epsilon = 1e-08
learn_rate = 0.02
decay_rate = 0.1
clip_limit = 0.002
norm_epsilon = 1e-06
masked_score = -1e30
bfloat = jnp.bfloat16
single = jnp.float32


def swap(values, axis, bit=0):
    count = lax.axis_size(axis)
    return lax.ppermute(values, axis, [(i, i ^ (1 << bit)) for i in range(count)])


def dp_bits():
    return lax.axis_size("dp").bit_length() - 1


def step(values, which):
    return swap(values, "mx") if which == "x" else swap(values, "dp", which)


def gather_dp(values):
    values = values[None]
    for bit in range(dp_bits()):
        values = jnp.concatenate([values, swap(values, "dp", bit)], axis=0)
    return values


def sum_dp(values):
    for bit in range(dp_bits()):
        values = values + swap(values, "dp", bit)
    return values


def sum_mp(values):
    values = values + swap(values, "mc")
    return values + swap(values, "mx")


def pair(values, axis, name):
    other = swap(values, name)
    first = lax.axis_index(name) == 0
    return jnp.stack([jnp.where(first, values, other), jnp.where(first, other, values)], axis=axis)


def tie(*values):
    return lax.optimization_barrier(values)


def high():
    return lax.axis_size("dp") // 2


def shift(values, by):
    count = lax.axis_size("dp")
    return lax.ppermute(values, "dp", [(i, (i + 2 * by) % count) for i in range(count)])


class Gather:
    def __init__(self, chunk=None):
        self.ring, self.pieces, self.done, self.got = [chunk], None, [], None

    def send_ring(self):
        last = len(self.ring) == 3
        for _ in range(high() - 4 if last else 0):
            self.ring.append(shift(self.ring[-1], 1))
        self.got = shift(self.ring[-1], 1)

    def closed(self):
        return len(self.ring) == high()

    def send(self, which):
        self.done.append(which)
        self.got = step(self.pieces, which)

    def take(self, got):
        if self.pieces is not None:
            self.pieces = jnp.stack([self.pieces, got])
            return
        self.ring.append(got)
        if self.closed():
            self.pieces = jnp.stack(self.ring)

    def parts(self, count):
        size = self.pieces.shape[1] // count
        cuts = tie(*(self.pieces[:, i * size : (i + 1) * size] for i in range(count)))
        parts = [Gather() for _ in cuts]
        for part, pieces in zip(parts, cuts):
            part.pieces = pieces
        return parts

    def units(self, first, last):
        part = Gather()
        part.pieces = lax.slice_in_dim(self.pieces, first, last, axis=2)
        return part

    def laid(self):
        x, y = (0, 1) if self.done[-1] == "x" else (1, 0)
        pieces = jnp.transpose(self.pieces, [3, x, 4, 2, y, 5, 6])
        return pieces.reshape(pieces.shape[0], -1, D)


class Scatter:
    def __init__(self, pieces):
        self.pieces, self.got, self.steps = pieces, None, 0

    def send(self, which):
        self.got = step(self.pieces[1], which)

    def send_ring(self):
        if self.steps == 2:
            self.sum = self.pieces[1]
        last = self.steps == 4
        for _ in range(high() - 4 if last else 0):
            self.got = shift(self.sum, 1)
            self.add_ring(self.got)
        self.got = shift(self.sum, 1)

    def add_ring(self, got):
        self.steps += 1
        own = self.pieces[(self.steps - 1) % high()]
        self.sum = (own.astype(single) + got.astype(single)).astype(bfloat)

    def take(self, got):
        if self.steps < 2:
            self.steps += 1
            self.pieces = (self.pieces[0].astype(single) + got.astype(single)).astype(bfloat)
        else:
            self.add_ring(got)

    def join(self, other):
        both = Scatter(jnp.concatenate([self.pieces, other.pieces], axis=1))
        both.steps = 2
        return both


def cut_units(grads, x_first):
    count, rows, depth = grads.shape
    pieces = grads.astype(bfloat).reshape(count, 2, 3, high(), 2, -1, depth)
    perm = [1, 4, 3, 0, 2, 5, 6] if x_first else [4, 1, 3, 0, 2, 5, 6]
    return jnp.transpose(pieces, perm)


def cut_far(grads, tail, x_first):
    pieces = grads.astype(bfloat).reshape((high(), 2, 2, 4) + tail)
    perm = [1, 2, 0, 3, 4, 5, 6] if x_first else [2, 1, 0, 3, 4, 5, 6]
    return jnp.transpose(pieces, perm)


def land(anchor, *streams):
    held = tie(anchor, *(stream.got for stream in streams))
    for stream, got in zip(streams, held[1:]):
        stream.take(got)
    return held[0]


WHOLE = pl.BlockSpec(memory_space=pltpu.VMEM)


def pick_kernel(ids, source, *targets):
    first = 0
    for target in targets:

        @pl.loop(0, target.shape[0])
        def _(i, first=first, target=target):
            target[i] = source[ids[first + i]]

        first += target.shape[0]


def pick_blocks(source, ids, counts):
    return pl.pallas_call(
        pick_kernel,
        out_shape=[
            jax.ShapeDtypeStruct((size,) + source.shape[1:], source.dtype) for size in counts
        ],
        grid_spec=pltpu.PrefetchScalarGridSpec(
            num_scalar_prefetch=1,
            grid=(),
            in_specs=[WHOLE],
            out_specs=[WHOLE] * len(counts),
        ),
        compiler_params=pltpu.CompilerParams(vmem_limit_bytes=40 << 20),
    )(ids.astype(jnp.int32), source)


def place_kernel(n_in, sizes, to, *refs):
    first = 0
    for source in refs[:n_in]:

        @pl.loop(0, source.shape[0])
        def _(i, first=first, source=source):
            unit = to[first + i]
            start = 0
            for target, size in zip(refs[n_in:], sizes):

                @pl.when((unit >= start) & (unit < start + size))
                def _(start=start, target=target):
                    target[unit - start] = source[i]

                start += size

        first += source.shape[0]


def place_blocks(sources, to, sizes):
    tail = sources[0].shape[1:]
    return pl.pallas_call(
        functools.partial(place_kernel, len(sources), sizes),
        out_shape=[jax.ShapeDtypeStruct((size,) + tail, sources[0].dtype) for size in sizes],
        grid_spec=pltpu.PrefetchScalarGridSpec(
            num_scalar_prefetch=1,
            grid=(),
            in_specs=[WHOLE] * len(sources),
            out_specs=[WHOLE] * len(sizes),
        ),
        compiler_params=pltpu.CompilerParams(vmem_limit_bytes=40 << 20),
    )(to.astype(jnp.int32), *sources)


def route_kernel(count, slots, ids, source, square, *targets):
    lane = lax.broadcasted_iota(jnp.int32, targets[0].shape[1:], 1)
    rest = square[0:1, 0:1]
    parts = []
    for _ in range(3):
        parts.append(rest.astype(bfloat).astype(single))
        rest = rest - parts[-1]
    told = jnp.where(lane < 128, parts[0], jnp.where(lane < 256, parts[1], parts[2]))
    for k, target in enumerate(targets):
        for s in range(slots):
            for h in range(3):
                target[3 * s + h] = source[ids[k * slots + s], h]
        target[3 * slots] = told.astype(bfloat)


def route_blocks(source, ids, square, count):
    slots = ids.shape[0] // count
    shape = (3 * slots + 1,) + source.shape[2:]
    return pl.pallas_call(
        functools.partial(route_kernel, count, slots),
        out_shape=[jax.ShapeDtypeStruct(shape, source.dtype)] * count,
        grid_spec=pltpu.PrefetchScalarGridSpec(
            num_scalar_prefetch=1,
            grid=(),
            in_specs=[WHOLE, WHOLE],
            out_specs=[WHOLE] * count,
        ),
        compiler_params=pltpu.CompilerParams(vmem_limit_bytes=40 << 20),
    )(ids.astype(jnp.int32), source, square)


def exchange_dp(blocks, before=None):
    count = lax.axis_size("dp")
    if count != 8 and before is not None:
        return exchange_dp(blocks), before()
    if count != 8:
        relative = jnp.arange(count) ^ lax.axis_index("dp")
        ranked = pick_blocks(jnp.stack(blocks), relative, (count,))[0]
        got = lax.all_to_all(ranked, "dp", 0, 0, tiled=True)
        got = pick_blocks(got, relative, (count,))[0]
        return [got.reshape((-1,) + got.shape[2:])]
    got = [blocks[0]] * count
    blocks = list(blocks)
    value = None
    for k in (7, 6, 5, 4, 1, 2, 3):
        if k == 1 and before is not None:
            value, *blocks[1:4] = tie(before(), *blocks[1:4])
        got[k] = lax.ppermute(blocks[k], "dp", [(i, i ^ k) for i in range(count)])
    return got if before is None else (got, value)


def adamw(weight, moment, square, grad, first_fix, second_fix):
    moment = beta_first * moment + (1.0 - beta_first) * grad
    square = beta_second * square + (1.0 - beta_second) * grad * grad
    update = (moment * first_fix) / (
        jnp.sqrt(square * second_fix) + adam_epsilon
    ) + decay_rate * weight
    return (weight - learn_rate * update, moment, square)


def adam_kernel(n_src, me, kind, scalars, *refs):
    routed, told, refs = refs[:n_src], refs[n_src : 2 * n_src], refs[2 * n_src :]
    slot_out, slot_in, weight, moment, square, latent_grad, *refs = refs
    latents, (new_weight, new_moment, new_square), refs = refs[:3], refs[3:6], refs[6:]
    new_latents, norm_out, grads = refs[:3], refs[3], refs[4]
    per, rows = routed[0].shape[0], routed[0].shape[2]
    squares = []
    for item in told:
        for j in range(per):
            parts = [item[j, 0, 0:1, 128 * i : 128 * i + 1].astype(single) for i in range(3)]
            squares.append(parts[0] + parts[1] + parts[2])
    while len(squares) > 1:
        squares = [squares[i] + squares[i + 1] for i in range(0, len(squares), 2)]
    norm = jnp.sqrt(squares[0] + scalars[0])
    factor = clip_limit / jnp.maximum(norm, clip_limit)

    @pl.when(pl.program_id(0) == 0)
    def _():
        norm_out[...] = jnp.broadcast_to(norm, norm_out.shape)
        held = [item[...] for item in latents]
        fresh = adamw(*held, latent_grad[...] * factor[None], scalars[1], scalars[2])
        for target, item in zip(new_latents, fresh):
            target[...] = item

    for i in range(n_src):
        for j in range(per):
            at = pl.multiple_of(((i * per + j) ^ me[0]) * rows, rows)
            for h in range(3):
                grads[h, pl.ds(at, rows), :] = routed[i][j, h].astype(single)
    sort = kind[pl.program_id(0)]
    for h in range(3):
        thin = lax.dot_general(
            slot_out[0, h], slot_in[0], (((0,), (0,)), ((), ())), preferred_element_type=single
        )
        grad = jnp.where(sort == 1, grads[h], thin) * factor
        w, m, v = weight[0, h], moment[0, h], square[0, h]
        fresh_w, fresh_m, fresh_v = adamw(w, m, v, grad, scalars[1], scalars[2])
        new_weight[0, h] = jnp.where(sort == 0, w, fresh_w)
        new_moment[0, h] = jnp.where(sort == 0, m, fresh_m)
        new_square[0, h] = jnp.where(sort == 0, v, fresh_v)


def adam_places(me, kind, scalars, routed, slot_out, slot_in, held, latent_grad, latents):
    slots, width, depth = held[0].shape
    head = width // 3
    clips = slot_in.shape[1]
    rows = routed[0].shape[1]
    routed = [item.reshape((-1, 3 * slots + 1, rows, depth)) for item in routed]
    per = routed[0].shape[0]
    big = pl.BlockSpec((1, 3, head, depth), lambda s, *_: (s, 0, 0, 0))
    latents_shape = (latent_grad.shape[1], 2, depth)
    small = pl.BlockSpec(latents_shape, lambda s, *_: (0, 0, 0))
    out = pl.pallas_call(
        functools.partial(adam_kernel, len(routed)),
        out_shape=[jax.ShapeDtypeStruct((slots, 3, head, depth), single)] * 3
        + [jax.ShapeDtypeStruct(latents_shape, single) for _ in latents]
        + [jax.ShapeDtypeStruct((8, 128), single)],
        grid_spec=pltpu.PrefetchScalarGridSpec(
            num_scalar_prefetch=3,
            grid=(slots,),
            in_specs=[pl.BlockSpec((per, 3, rows, depth), lambda s, *_: (0, s, 0, 0))]
            * len(routed)
            + [pl.BlockSpec((per, 1, rows, depth), lambda s, *_: (0, 3 * slots, 0, 0))]
            * len(routed)
            + [
                pl.BlockSpec((1, 3, clips, head), lambda s, *_: (s, 0, 0, 0)),
                pl.BlockSpec((1, clips, depth), lambda s, *_: (s, 0, 0)),
                big,
                big,
                big,
            ]
            + [small] * 4,
            out_specs=[big] * 3 + [small] * 3 + [pl.BlockSpec((8, 128), lambda s, *_: (0, 0))],
            scratch_shapes=[pltpu.VMEM((3, head, depth), single)],
        ),
        compiler_params=pltpu.CompilerParams(vmem_limit_bytes=60 << 20),
    )(
        me,
        kind,
        scalars,
        *routed,
        *routed,
        slot_out.reshape(slots, clips, 3, head).swapaxes(1, 2),
        slot_in,
        *(item.reshape(slots, 3, head, depth) for item in held),
        latent_grad.swapaxes(0, 1),
        *(item.swapaxes(0, 1) for item in latents),
    )
    places = [item.reshape(slots, width, depth) for item in out[:3]]
    return places + [item.swapaxes(0, 1) for item in out[3:6]] + [out[6][0, 0]]


def normed(values):
    center = values - jnp.mean(values, axis=-1, keepdims=True)
    spread_sq = jnp.mean(center * center, axis=-1, keepdims=True)
    return center * lax.rsqrt(spread_sq + norm_epsilon)


def modulate(values, shift, scale):
    return normed(values) * (1.0 + scale[None, :]) + shift[None, :]


def modulate_back(values, shift, scale, grad):
    _, pullback = jax.vjp(modulate, values, shift, scale)
    return pullback(grad)


def sinusoid(timestep):
    half_width = D // 2
    frequency = jnp.exp(-math.log(10000.0) * jnp.arange(half_width).astype(single) / half_width)
    angles = timestep.astype(single)[:, None] * frequency[None, :]
    return jnp.concatenate([jnp.cos(angles), jnp.sin(angles)], axis=1)


def matmul(form, left, right):
    return jnp.einsum(form, left, right, preferred_element_type=single)


NT_DIMS = (((1,), (1,)), ((), ()))
TN_DIMS = (((0,), (0,)), ((), ()))


def dot(left, right, dims=(((1,), (0,)), ((), ()))):
    return lax.dot_general(left, right, dims, preferred_element_type=single)


def scores_of(keys, query, length):
    scores = dot(keys, query, NT_DIMS) * HD ** (-0.5)
    if length is None:
        return scores
    row = lax.broadcasted_iota(jnp.int32, scores.shape, 0)
    return jnp.where(row < length, scores, masked_score)


def attend_kernel(masked, length, query, keys, values, output, totals):
    limit = length[0] if masked else None
    rows = []
    for h in range(2):
        at = slice(h * HD, (h + 1) * HD)
        scores = scores_of(keys[:, at], query[:, at], limit)
        top = jnp.max(scores, axis=0, keepdims=True)
        shifted = jnp.exp(scores - top)
        total = jnp.sum(shifted, axis=0, keepdims=True)
        probs = (shifted * (1.0 / total)).astype(bfloat)
        rows.append(dot(values[:, at], probs, TN_DIMS))
        totals[0, h : h + 1, :] = top + jnp.log(total)
    output[...] = jnp.concatenate(rows, axis=0).T.astype(bfloat)


def attend_back_kernel(masked, length, query, keys, values, grad_out, totals, dq, dk, dv):
    limit = length[0] if masked else None
    query_rows, key_cols, value_cols = [], [], []
    for h in range(2):
        at = slice(h * HD, (h + 1) * HD)
        q, k, v, do = query[:, at], keys[:, at], values[:, at], grad_out[:, at]
        probs = jnp.exp(scores_of(k, q, limit) - totals[0, h : h + 1, :])
        grad_probs = dot(v, do, NT_DIMS)
        inner = jnp.sum(probs * grad_probs, axis=0, keepdims=True)
        grad_scores = (probs * (grad_probs - inner)).astype(bfloat)
        query_rows.append(dot(k, grad_scores, TN_DIMS))
        key_cols.append(dot(grad_scores, q))
        value_cols.append(dot(probs.astype(bfloat), do))
    scale = HD ** (-0.5)
    dq[...] = (jnp.concatenate(query_rows, axis=0).T * scale).astype(bfloat)
    dk[...] = (jnp.concatenate(key_cols, axis=1) * scale).astype(bfloat)
    dv[...] = jnp.concatenate(value_cols, axis=1).astype(bfloat)


def pair_call(kernel, length, ins, outs, flops):
    def spec(shape):
        if len(shape) == 3:
            return pl.BlockSpec((1,) + shape[1:], lambda i, *_: (i, 0, 0))
        return pl.BlockSpec((shape[0], 2 * HD), lambda i, *_: (0, i))

    masked = length is not None
    length = jnp.zeros((1,), jnp.int32) if length is None else length.reshape(1)
    return pl.pallas_call(
        functools.partial(kernel, masked),
        out_shape=outs,
        grid_spec=pltpu.PrefetchScalarGridSpec(
            num_scalar_prefetch=1,
            grid=(ins[0].shape[1] // (2 * HD),),
            in_specs=[spec(item.shape) for item in ins],
            out_specs=[spec(item.shape) for item in outs],
        ),
        compiler_params=pltpu.CompilerParams(vmem_limit_bytes=48 << 20),
        cost_estimate=pl.CostEstimate(
            flops=flops, bytes_accessed=8 << 20, transcendentals=6 * FRAMES * FRAMES
        ),
    )(length, *ins)


def attention(query, keys, values, length):
    shape = query.shape
    outs = [
        jax.ShapeDtypeStruct(shape, bfloat),
        jax.ShapeDtypeStruct((shape[1] // (2 * HD), 2, shape[0]), single),
    ]
    flops = 16 * shape[0] * keys.shape[0] * shape[1]
    return pair_call(attend_kernel, length, (query, keys, values), outs, flops)


def attention_back(query, keys, values, length, grad_out, totals):
    outs = [jax.ShapeDtypeStruct(item.shape, bfloat) for item in (query, keys, values)]
    flops = 40 * query.shape[0] * keys.shape[0] * query.shape[1]
    ins = (query, keys, values, grad_out, totals)
    return pair_call(attend_back_kernel, length, ins, outs, flops)


def spread(values):
    return jnp.concatenate([values, swap(values, "mc")], axis=0)


def collect(left, right):
    own = left.shape[0] // 2
    other = matmul("fk,kd->fd", left[own:], right).astype(bfloat)
    got = swap(other, "mc")
    return matmul("fk,kd->fd", left[:own], right) + got.astype(single)


def body(
    clean_latent,
    noise_draw,
    captions,
    caption_len,
    timestep,
    step_weight,
    step_count,
    unit_slot,
    master,
    first_moment,
    second_moment,
    latent_master,
    latent_first,
    latent_second,
):
    slots = master.shape[0]
    width = master.shape[1]
    n_dp = lax.axis_size("dp")
    index = lax.axis_index("dp")
    column = 2 * lax.axis_index("mx") + lax.axis_index("mc")
    clip = lax.axis_index("mx")
    clips = captions.shape[0]
    owner = unit_slot // slots
    place = unit_slot % slots
    local_ids = index * slots + jnp.arange(slots)
    pick = unit_slot[None, :] == local_ids[:, None]
    live_slot = jnp.any(pick, axis=1)

    table = jnp.arange(step_weight.shape[0])
    clip_weight = jnp.sum(
        jnp.where(timestep[:, None] == table[None, :], step_weight[None, :], 0.0), axis=1
    )
    cap_mask = jnp.arange(captions.shape[1])[None, :] < caption_len[:, None]
    pooled = (
        jnp.sum(jnp.where(cap_mask[:, :, None], captions.astype(single), 0.0), axis=1)
        / caption_len.astype(single)[:, None]
    )
    packed = jnp.concatenate(
        [sinusoid(timestep), pooled, jnp.broadcast_to(clip_weight[:, None], (clips, 128))], axis=1
    )

    master_low = master.astype(bfloat)
    split = master_low.reshape(slots, 3, n_dp, width // (3 * n_dp), D)
    blocks = [
        lax.dynamic_index_in_dim(split, index ^ k, 2, keepdims=False) for k in range(n_dp)
    ]
    def gather_packed():
        values = packed
        for i, bit in enumerate(reversed(range(dp_bits()))):
            values = jnp.stack([values, swap(values, "dp", bit)], axis=i)
        return values.reshape(n_dp * clips, -1)

    got, packed = exchange_dp(blocks, gather_packed)

    sinus_low = packed[:, :D].astype(bfloat)
    pooled_low = packed[:, D : 2 * D].astype(bfloat)
    weight_total = jnp.sum(packed[:, 2 * D])

    def held(u):
        return lax.dynamic_index_in_dim(master_low, place[u], 0, keepdims=False)

    zero = jnp.zeros((), bfloat)
    cond_part = matmul(
        "bd,ed->be", jnp.where(owner[24] == index, sinus_low, zero), held(24)
    ) + matmul("bd,ed->be", jnp.where(owner[25] == index, pooled_low, zero), held(25))
    row = jnp.arange(n_dp * clips)
    reorder = (row[:, None] ^ (index * clips)) == row[None, :]
    reorder = reorder.astype(single)

    def reordered(values):
        return jnp.einsum("bc,cd->bd", reorder, values, precision=highest)

    cond_part = pair(reordered(cond_part), 1, "mx")
    cond_part, *got = tie(cond_part, *got)
    unit_of = jnp.sum(
        jnp.where(
            unit_slot[None, :] == jnp.arange(n_dp * slots)[:, None],
            jnp.arange(UNITS)[None, :] + 1,
            0,
        ),
        axis=1,
    ) - 1
    table = jnp.stack(
        [
            unit_of.reshape(n_dp, slots)[jnp.array([d ^ k for k in range(n_dp)])]
            for d in range(n_dp)
        ]
    )
    unit_at = lax.dynamic_index_in_dim(table, index, 0, keepdims=False).reshape(-1)
    chunk_near, chunk_cross, chunk_up, chunk_down = place_blocks(got, unit_at, (4, 4, 4, 4))
    unit_tail = chunk_near.shape[1:]
    chunk_near, chunk_up, chunk_down, cond_part = tie(
        chunk_near, chunk_up, chunk_down, cond_part
    )
    near, cross = Gather(chunk_near), Gather(chunk_cross)
    near.send_ring()
    got_up, got_down = swap(chunk_up, "dp", 0), swap(chunk_down, "mx")
    cond_part = pair(cond_part, 2, "mc").reshape(n_dp * clips, D)
    for bit in range(dp_bits()):
        cond_part = cond_part + swap(cond_part, "dp", bit)
        if bit < 3:
            cond_part = land(cond_part, near)
            if bit < 2:
                near.send_ring()
        if bit == 1:
            cond_part, got_up, got_down = tie(cond_part, got_up, got_down)
    far = Gather(jnp.stack([chunk_up, got_up, chunk_down, got_down]).reshape((2, 2, 4) + unit_tail))
    cond = tie(reordered(cond_part))[0]
    active = jax.nn.silu(cond).astype(bfloat)
    all_rows = matmul("bd,sed->bse", active, master_low)
    ada = pick[:, 16:24]
    rows = jnp.einsum("sj,bse->bje", ada.astype(single), all_rows, precision=highest)
    rows = rows.reshape(n_dp, clips, 8, width)
    near_a, near_b = near.parts(2)
    rows, near_a.pieces, near_b.pieces, cross.ring[0] = tie(
        rows, near_a.pieces, near_b.pieces, cross.ring[0]
    )
    near_a.send(0)
    near_b.send("x")
    cross.send_ring()
    for bit in reversed(range(1, dp_bits())):
        half = rows.shape[0] // 2
        rows = rows[:half] + swap(rows[half:], "dp", bit)
        if bit == 2:
            rows = land(rows, near_a, near_b, cross)
            near_a.send("x")
            near_b.send(0)
            cross.send_ring()
    rows = land(rows, cross)
    rows, far.ring[0] = tie(rows, far.ring[0])
    cross.send_ring()
    far.send_ring()
    mine = lax.dynamic_index_in_dim(rows, clip, 1, keepdims=False)
    theirs = swap(lax.dynamic_index_in_dim(rows, 1 - clip, 1, keepdims=False), "mx")
    rows = jnp.stack(
        [jnp.where(clip == 0, mine, theirs), jnp.where(clip == 0, theirs, mine)], axis=2
    )
    rows = land(rows, near_a, near_b, cross)
    rows = rows[0] + swap(rows[1], "dp", 0)
    cross_a, cross_b = cross.parts(2)
    rows, cross_a.pieces, cross_b.pieces = tie(rows, cross_a.pieces, cross_b.pieces)
    rows = land(rows, far)
    cross_a.send(0)
    cross_b.send("x")
    far.send_ring()
    modulation = tie(pair(rows, 2, "mc").reshape(8, D))[0]

    text = lax.dynamic_index_in_dim(captions, clip, 0, keepdims=False)
    text_len = lax.dynamic_index_in_dim(caption_len, clip, 0, keepdims=False)
    my_step = lax.dynamic_index_in_dim(timestep, clip, 0, keepdims=False)
    my_weight = lax.dynamic_index_in_dim(clip_weight, clip, 0, keepdims=False)
    latents = jnp.stack([clean_latent, noise_draw], axis=1)
    away = swap(lax.dynamic_index_in_dim(latents, 1 - clip, 0, keepdims=False), "mx")
    latents = jnp.concatenate(
        [lax.dynamic_index_in_dim(latents, clip, 0, keepdims=False), away], axis=1
    )
    level = (my_step.astype(single) + 0.5) / NT
    noisy = (1.0 - level) * latents[0] + level * latents[1]
    target = latents[1] - latents[0]

    hidden_zero = jnp.einsum("fc,cd->fd", noisy, latent_master[0], precision=highest)
    first_in = spread(modulate(hidden_zero, modulation[0], modulation[1]).astype(bfloat))
    w_self = jnp.concatenate([near_a.laid(), near_b.laid()], axis=0)
    self_query, self_keys, self_values = (
        matmul("fd,ed->fe", first_in, w_self[u]).astype(bfloat) for u in range(3)
    )
    self_flat, self_total = attention(self_query, self_keys, self_values, None)
    self_flat = land(self_flat, cross_a, cross_b, far)
    cross_a.send("x")
    cross_b.send(0)
    far.send_ring()
    self_branch = collect(self_flat, w_self[3])
    hidden_one = hidden_zero + modulation[2] * self_branch
    second_in = spread(normed(hidden_one).astype(bfloat))
    second_in = land(second_in, cross_a, cross_b, far)
    ups, downs = far.parts(2)
    ups.pieces, downs.pieces = ups.pieces[:, 0], downs.pieces[:, 0]
    last = []
    for i in range(2):
        last += [ups.units(2 * i, 2 * i + 2), downs.units(2 * i, 2 * i + 2)]
    cuts = tie(*(item.pieces for item in last))
    for item, pieces in zip(last, cuts):
        item.pieces = pieces
    last[0].send("x")
    last[1].send(0)
    w_cross = jnp.concatenate([cross_a.laid(), cross_b.laid()], axis=0)
    weights = [w_self[i] for i in range(4)] + [w_cross[i] for i in range(4)]
    cross_query = matmul("fd,ed->fe", second_in, weights[4]).astype(bfloat)
    cross_keys = matmul("ld,ed->le", text, weights[5]).astype(bfloat)
    cross_values = matmul("ld,ed->le", text, weights[6]).astype(bfloat)
    cross_flat, cross_total = attention(cross_query, cross_keys, cross_values, text_len)
    cross_flat, *far_got = tie(cross_flat, last[0].got, last[1].got)
    cross_flat, last[2].pieces, last[3].pieces = tie(
        cross_flat, last[2].pieces, last[3].pieces
    )
    last[2].send("x")
    last[3].send(0)
    cross_branch = collect(cross_flat, weights[7])
    hidden_two = hidden_one + cross_branch
    third_in = spread(modulate(hidden_two, modulation[3], modulation[4]).astype(bfloat))
    third_in, *more = tie(third_in, last[2].got, last[3].got)
    far_got += more
    w_up, w_down = (
        jnp.concatenate(
            [jnp.stack([last[i].pieces, far_got[i]], axis=axis) for i in (part, part + 2)], axis=3
        ).reshape(-1, D)
        for part, axis in ((0, 1), (1, 2))
    )
    upper = matmul("fd,kd->fk", third_in, w_up).astype(bfloat)
    upper_wide = upper.astype(single)
    activated = jax.nn.gelu(upper_wide, approximate=True).astype(bfloat)
    mlp_branch = collect(activated, w_down)
    hidden_three = hidden_two + modulation[5] * mlp_branch
    final_wide = modulate(hidden_three, modulation[6], modulation[7]).astype(bfloat).astype(single)
    predicted = jnp.einsum("fd,cd->fc", final_wide, latent_master[1], precision=highest)
    error = predicted - target
    loss_local = jnp.sum(my_weight * error * error)

    grad_pred = 2.0 / (C * FRAMES) * my_weight * error / weight_total
    grad_out_proj = jnp.einsum("fc,fd->cd", grad_pred, final_wide, precision=highest)
    grad_final = jnp.einsum("fc,cd->fd", grad_pred, latent_master[1], precision=highest)
    grad_three, shift_f, scale_f = modulate_back(
        hidden_three, modulation[6], modulation[7], grad_final
    )
    gate_m_grad = jnp.sum(grad_three * mlp_branch, axis=0)
    grad_mlp = spread((modulation[5] * grad_three).astype(bfloat))
    grad_w_down = matmul("fk,fd->kd", activated, grad_mlp)
    down = Scatter(cut_far(grad_w_down, unit_tail, True))
    grad_mlp, down.pieces = tie(grad_mlp, down.pieces)
    down.send("x")
    grad_act = matmul("fd,kd->fk", grad_mlp, w_down)
    _, gelu_back = jax.vjp(lambda inner_in: jax.nn.gelu(inner_in, approximate=True), upper_wide)
    grad_upper = gelu_back(grad_act)[0].astype(bfloat)
    grad_w_up = matmul("fk,fd->kd", grad_upper, third_in)
    up = Scatter(cut_far(grad_w_up, unit_tail, False))
    up.send(0)
    grad_third = collect(grad_upper, w_up)
    grad_two, shift_m, scale_m = modulate_back(hidden_two, modulation[3], modulation[4], grad_third)
    grad_two = grad_two + grad_three
    grad_cross = spread(grad_two.astype(bfloat))
    grad_cross_flat = matmul("fd,kd->fk", grad_cross, weights[7]).astype(bfloat)
    grad_w_cross_out = matmul("fk,fd->kd", cross_flat, grad_cross)
    cq_grad, ck_grad, cv_grad = attention_back(
        cross_query, cross_keys, cross_values, text_len, grad_cross_flat, cross_total
    )
    cq_grad = land(cq_grad, down, up)
    down.send(0)
    up.send("x")
    grad_w_cq = matmul("fk,fd->kd", cq_grad, second_in)
    grad_w_ck = matmul("lk,ld->kd", ck_grad, text)
    grad_w_cv = matmul("lk,ld->kd", cv_grad, text)
    cross_a = Scatter(cut_units(jnp.stack([grad_w_cq, grad_w_ck]), True))
    cross_b = Scatter(cut_units(jnp.stack([grad_w_cv, grad_w_cross_out]), False))
    cross_a.send("x")
    cross_b.send(0)
    grad_second = collect(cq_grad, weights[4])
    _, norm_back = jax.vjp(normed, hidden_one)
    grad_one = grad_two + norm_back(grad_second)[0]
    gate_a_grad = jnp.sum(grad_one * self_branch, axis=0)
    grad_self = spread((modulation[2] * grad_one).astype(bfloat))
    grad_self_flat = matmul("fd,kd->fk", grad_self, weights[3]).astype(bfloat)
    grad_self_flat = land(grad_self_flat, down, up)
    far = up.join(down)
    far.send_ring()
    grad_w_self_out = matmul("fk,fd->kd", self_flat, grad_self)
    self_grads = attention_back(
        self_query, self_keys, self_values, None, grad_self_flat, self_total
    )
    self_grads = jnp.concatenate(self_grads, axis=1)
    self_grads = land(self_grads, cross_a, cross_b, far)
    far.send_ring()
    cross_a.send(0)
    cross_b.send("x")
    grad_w_attn = matmul("fk,fd->kd", self_grads, first_in)
    grad_w_attn = land(grad_w_attn, far)
    far.send_ring()
    near_a = Scatter(cut_units(grad_w_attn[: 4 * width].reshape(2, 2 * width, D), True))
    near_b = Scatter(cut_units(jnp.stack([grad_w_attn[4 * width :], grad_w_self_out]), False))
    near_a.send("x")
    near_b.send(0)
    grad_first = collect(self_grads, jnp.concatenate(weights[0:3], axis=0))
    grad_first = land(grad_first, cross_a, cross_b)
    cross = cross_a.join(cross_b)
    cross.send_ring()
    grad_zero, shift_a, scale_a = modulate_back(
        hidden_zero, modulation[0], modulation[1], grad_first
    )
    grad_zero = land(grad_zero, near_a, near_b, cross, far)
    cross.send_ring()
    near_a.send(0)
    near_b.send("x")
    grad_zero = grad_zero + grad_one
    grad_in_proj = jnp.einsum("fc,fd->cd", noisy, grad_zero, precision=highest)

    grad_mod = jnp.stack(
        [shift_a, scale_a, gate_a_grad, shift_m, scale_m, gate_m_grad, shift_f, scale_f], axis=0
    )
    grad_mod = (grad_mod + swap(grad_mod, "mc")).astype(bfloat)
    for i, bit in enumerate(reversed(range(1, dp_bits()))):
        grad_mod = jnp.stack([grad_mod, swap(grad_mod, "dp", bit)], axis=i)
        if i == 0:
            grad_mod = land(grad_mod, near_a, near_b, cross)
            near = near_a.join(near_b).pieces
            z_got = [shift(near[j], -j) for j in range(1, high())]
            cross.send_ring()
    grad_mod = pair(grad_mod, dp_bits() - 1, "mx")
    grad_mod = jnp.stack([grad_mod, swap(grad_mod, "dp", 0)], axis=dp_bits() - 1)
    grad_mod = tie(grad_mod.reshape(n_dp * clips, 8, D))[0]
    mod_cols = lax.dynamic_index_in_dim(
        grad_mod.reshape(n_dp * clips, 8, D // width, width), column, 2, keepdims=False
    )
    slot_mod = matmul("sj,bje->sbe", ada.astype(bfloat), mod_cols).astype(bfloat)
    grad_active = matmul("sbe,sed->bd", slot_mod, master_low)
    small = jnp.concatenate([grad_in_proj, grad_out_proj], axis=0)
    pad = jnp.full((2 * C, 128), loss_local, single)
    mixed = jnp.concatenate(
        [
            jnp.pad(reordered(grad_active), ((0, 0), (0, 128))),
            jnp.concatenate([small, pad], axis=1),
        ],
        axis=0,
    )
    mixed = sum_mp(mixed)
    total = near[0].astype(single)
    for item in z_got:
        total = total + item.astype(single)
    cross.take(cross.got)
    reduced = [total] + [item.sum.astype(single) for item in (cross, far)]
    reduced = jnp.concatenate(reduced, axis=0)
    wide_square = sum_mp(jnp.broadcast_to(jnp.sum(reduced * reduced), (8, 128)))
    wide_at = jnp.where((unit_at >= 0) & (unit_at < WIDE), unit_at, 0)
    wide_square, mixed = tie(wide_square, mixed)
    mixed = sum_dp(mixed)
    grad_active, small = reordered(mixed[: n_dp * clips, :D]), mixed[n_dp * clips :]
    latent_grad = small[:, :D].reshape(2, C, D)
    loss_sum = small[0, D]
    routes = route_blocks(reduced.astype(bfloat), wide_at, wide_square, n_dp)
    routed = exchange_dp(routes)
    _, silu_back = jax.vjp(jax.nn.silu, cond)
    grad_cond = silu_back(grad_active)[0].astype(bfloat)
    cond_cols = lax.dynamic_index_in_dim(
        grad_cond.reshape(n_dp * clips, D // width, width), column, 1, keepdims=False
    )
    is_time, is_pool = pick[:, 24], pick[:, 25]
    slot_out = jnp.where((is_time | is_pool)[:, None, None], cond_cols[None], slot_mod)
    slot_in = jnp.where(
        is_time[:, None, None],
        sinus_low[None],
        jnp.where(is_pool[:, None, None], pooled_low[None], active[None]),
    )
    def gram(values):
        return matmul("bd,cd->bc", values, values)

    flat_mod = grad_mod.reshape(n_dp * clips, 8 * D)
    thin_square = jnp.sum(gram(active) * gram(flat_mod)) + jnp.sum(
        (gram(sinus_low) + gram(pooled_low)) * gram(grad_cond)
    )

    rest_square = thin_square + jnp.sum(latent_grad * latent_grad)
    count = step_count[0].astype(single)
    is_wide = jnp.any(pick[:, :WIDE], axis=1)
    kind = jnp.where(is_wide, 1, jnp.where(live_slot, 2, 0)).astype(jnp.int32)
    fixes = [1.0 / (1.0 - jnp.power(beta, count)) for beta in (beta_first, beta_second)]
    *outputs, grad_norm = adam_places(
        index.reshape(1).astype(jnp.int32),
        kind,
        jnp.stack([rest_square] + fixes),
        routed,
        slot_out,
        slot_in,
        (master, first_moment, second_moment),
        latent_grad,
        (latent_master, latent_first, latent_second),
    )
    loss_value = loss_sum / (C * FRAMES * weight_total)
    return (*outputs, grad_norm, loss_value)


def solution(mesh):
    n_dp, n_mp = mesh.shape["dp"], mesh.shape["mp"]
    fine = Mesh(mesh.devices.reshape(n_dp, n_mp // 2, 2), ("dp", "mx", "mc"))
    frames = P("dp", ("mx", "mc"), None)
    placed = (
        frames,
        frames,
        P("dp", None, None),
        P("dp"),
        P("dp"),
        P(),
        P(),
        P(),
        frames,
        frames,
        frames,
        P(),
        P(),
        P(),
    )
    return jax.shard_map(
        body,
        mesh=fine,
        in_specs=placed,
        out_specs=(frames, frames, frames, P(), P(), P(), P(), P()),
        check_vma=False,
    )
```

```python
import functools
import math

import jax
import jax.numpy as jnp
from jax import lax
from jax.experimental import pallas as pl
from jax.experimental.pallas import tpu as pltpu
from jax.sharding import Mesh
from jax.sharding import PartitionSpec as P

D = 768
HD = 64
C = 20
FRAMES = 768
NT = 1000
UNITS = 26
WIDE = 16

highest = lax.Precision.HIGHEST
beta_first = 0.9
beta_second = 0.999
adam_epsilon = 1e-08
learn_rate = 0.02
decay_rate = 0.1
clip_limit = 0.002
norm_epsilon = 1e-06
masked_score = -1e30
bfloat = jnp.bfloat16
single = jnp.float32


def swap(values, axis, bit=0):
    count = lax.axis_size(axis)
    return lax.ppermute(values, axis, [(i, i ^ (1 << bit)) for i in range(count)])


def dp_bits():
    return lax.axis_size("dp").bit_length() - 1


def step(values, which):
    return swap(values, "mx") if which == "x" else swap(values, "dp", which)


def gather_dp(values):
    values = values[None]
    for bit in range(dp_bits()):
        values = jnp.concatenate([values, swap(values, "dp", bit)], axis=0)
    return values


def sum_dp(values):
    for bit in range(dp_bits()):
        values = values + swap(values, "dp", bit)
    return values


def sum_mp(values):
    values = values + swap(values, "mc")
    return values + swap(values, "mx")


def pair(values, axis, name):
    other = swap(values, name)
    first = lax.axis_index(name) == 0
    return jnp.stack([jnp.where(first, values, other), jnp.where(first, other, values)], axis=axis)


def tie(*values):
    return lax.optimization_barrier(values)


def high():
    return lax.axis_size("dp") // 2


def shift(values, by):
    count = lax.axis_size("dp")
    return lax.ppermute(values, "dp", [(i, (i + 2 * by) % count) for i in range(count)])


class Gather:
    def __init__(self, chunk=None):
        self.ring, self.pieces, self.done, self.got = [chunk], None, [], None

    def send_ring(self):
        last = len(self.ring) == 3
        for _ in range(high() - 4 if last else 0):
            self.ring.append(shift(self.ring[-1], 1))
        self.got = shift(self.ring[-1], 1)

    def closed(self):
        return len(self.ring) == high()

    def send(self, which):
        self.done.append(which)
        self.got = step(self.pieces, which)

    def take(self, got):
        if self.pieces is not None:
            self.pieces = jnp.stack([self.pieces, got])
            return
        self.ring.append(got)
        if self.closed():
            self.pieces = jnp.stack(self.ring)

    def parts(self, count):
        size = self.pieces.shape[1] // count
        cuts = tie(*(self.pieces[:, i * size : (i + 1) * size] for i in range(count)))
        parts = [Gather() for _ in cuts]
        for part, pieces in zip(parts, cuts):
            part.pieces = pieces
        return parts

    def units(self, first, last):
        part = Gather()
        part.pieces = lax.slice_in_dim(self.pieces, first, last, axis=2)
        return part

    def laid(self):
        x, y = (0, 1) if self.done[-1] == "x" else (1, 0)
        pieces = jnp.transpose(self.pieces, [3, x, 4, 2, y, 5, 6])
        return pieces.reshape(pieces.shape[0], -1, D)


class Scatter:
    def __init__(self, pieces):
        self.pieces, self.got, self.steps = pieces, None, 0

    def send(self, which):
        self.got = step(self.pieces[1], which)

    def send_ring(self):
        if self.steps == 2:
            self.sum = self.pieces[1]
        last = self.steps == 4
        for _ in range(high() - 4 if last else 0):
            self.got = shift(self.sum, 1)
            self.add_ring(self.got)
        self.got = shift(self.sum, 1)

    def add_ring(self, got):
        self.steps += 1
        own = self.pieces[(self.steps - 1) % high()]
        self.sum = (own.astype(single) + got.astype(single)).astype(bfloat)

    def take(self, got):
        if self.steps < 2:
            self.steps += 1
            self.pieces = (self.pieces[0].astype(single) + got.astype(single)).astype(bfloat)
        else:
            self.add_ring(got)

    def join(self, other):
        both = Scatter(jnp.concatenate([self.pieces, other.pieces], axis=1))
        both.steps = 2
        return both


def cut_units(grads, x_first):
    count, rows, depth = grads.shape
    pieces = grads.astype(bfloat).reshape(count, 2, 3, high(), 2, -1, depth)
    perm = [1, 4, 3, 0, 2, 5, 6] if x_first else [4, 1, 3, 0, 2, 5, 6]
    return jnp.transpose(pieces, perm)


def cut_far(grads, tail, x_first):
    pieces = grads.astype(bfloat).reshape((high(), 2, 2, 4) + tail)
    perm = [1, 2, 0, 3, 4, 5, 6] if x_first else [2, 1, 0, 3, 4, 5, 6]
    return jnp.transpose(pieces, perm)


def land(anchor, *streams):
    held = tie(anchor, *(stream.got for stream in streams))
    for stream, got in zip(streams, held[1:]):
        stream.take(got)
    return held[0]


WHOLE = pl.BlockSpec(memory_space=pltpu.VMEM)


def pick_kernel(ids, source, *targets):
    first = 0
    for target in targets:

        @pl.loop(0, target.shape[0])
        def _(i, first=first, target=target):
            target[i] = source[ids[first + i]]

        first += target.shape[0]


def pick_blocks(source, ids, counts):
    return pl.pallas_call(
        pick_kernel,
        out_shape=[
            jax.ShapeDtypeStruct((size,) + source.shape[1:], source.dtype) for size in counts
        ],
        grid_spec=pltpu.PrefetchScalarGridSpec(
            num_scalar_prefetch=1,
            grid=(),
            in_specs=[WHOLE],
            out_specs=[WHOLE] * len(counts),
        ),
        compiler_params=pltpu.CompilerParams(vmem_limit_bytes=40 << 20),
    )(ids.astype(jnp.int32), source)


def place_kernel(n_in, sizes, to, *refs):
    first = 0
    for source in refs[:n_in]:

        @pl.loop(0, source.shape[0])
        def _(i, first=first, source=source):
            unit = to[first + i]
            start = 0
            for target, size in zip(refs[n_in:], sizes):

                @pl.when((unit >= start) & (unit < start + size))
                def _(start=start, target=target):
                    target[unit - start] = source[i]

                start += size

        first += source.shape[0]


def place_blocks(sources, to, sizes):
    tail = sources[0].shape[1:]
    return pl.pallas_call(
        functools.partial(place_kernel, len(sources), sizes),
        out_shape=[jax.ShapeDtypeStruct((size,) + tail, sources[0].dtype) for size in sizes],
        grid_spec=pltpu.PrefetchScalarGridSpec(
            num_scalar_prefetch=1,
            grid=(),
            in_specs=[WHOLE] * len(sources),
            out_specs=[WHOLE] * len(sizes),
        ),
        compiler_params=pltpu.CompilerParams(vmem_limit_bytes=40 << 20),
    )(to.astype(jnp.int32), *sources)


def route_kernel(count, slots, ids, source, square, *targets):
    lane = lax.broadcasted_iota(jnp.int32, targets[0].shape[1:], 1)
    rest = square[0:1, 0:1]
    parts = []
    for _ in range(3):
        parts.append(rest.astype(bfloat).astype(single))
        rest = rest - parts[-1]
    told = jnp.where(lane < 128, parts[0], jnp.where(lane < 256, parts[1], parts[2]))
    for k, target in enumerate(targets):
        for s in range(slots):
            for h in range(3):
                target[3 * s + h] = source[ids[k * slots + s], h]
        target[3 * slots] = told.astype(bfloat)


def route_blocks(source, ids, square, count):
    slots = ids.shape[0] // count
    shape = (3 * slots + 1,) + source.shape[2:]
    return pl.pallas_call(
        functools.partial(route_kernel, count, slots),
        out_shape=[jax.ShapeDtypeStruct(shape, source.dtype)] * count,
        grid_spec=pltpu.PrefetchScalarGridSpec(
            num_scalar_prefetch=1,
            grid=(),
            in_specs=[WHOLE, WHOLE],
            out_specs=[WHOLE] * count,
        ),
        compiler_params=pltpu.CompilerParams(vmem_limit_bytes=40 << 20),
    )(ids.astype(jnp.int32), source, square)


def exchange_dp(blocks, before=None):
    count = lax.axis_size("dp")
    if count != 8 and before is not None:
        return exchange_dp(blocks), before()
    if count != 8:
        relative = jnp.arange(count) ^ lax.axis_index("dp")
        ranked = pick_blocks(jnp.stack(blocks), relative, (count,))[0]
        got = lax.all_to_all(ranked, "dp", 0, 0, tiled=True)
        got = pick_blocks(got, relative, (count,))[0]
        return [got.reshape((-1,) + got.shape[2:])]
    got = [blocks[0]] * count
    blocks = list(blocks)
    value = None
    for k in (7, 6, 5, 4, 1, 2, 3):
        if k == 1 and before is not None:
            value, *blocks[1:4] = tie(before(), *blocks[1:4])
        got[k] = lax.ppermute(blocks[k], "dp", [(i, i ^ k) for i in range(count)])
    return got if before is None else (got, value)


def adamw(weight, moment, square, grad, first_fix, second_fix):
    moment = beta_first * moment + (1.0 - beta_first) * grad
    square = beta_second * square + (1.0 - beta_second) * grad * grad
    update = (moment * first_fix) / (
        jnp.sqrt(square * second_fix) + adam_epsilon
    ) + decay_rate * weight
    return (weight - learn_rate * update, moment, square)


def adam_kernel(n_src, me, kind, scalars, *refs):
    routed, told, refs = refs[:n_src], refs[n_src : 2 * n_src], refs[2 * n_src :]
    slot_out, slot_in, weight, moment, square, latent_grad, *refs = refs
    latents, (new_weight, new_moment, new_square), refs = refs[:3], refs[3:6], refs[6:]
    new_latents, norm_out, grads = refs[:3], refs[3], refs[4]
    per, rows = routed[0].shape[0], routed[0].shape[2]
    squares = []
    for item in told:
        for j in range(per):
            parts = [item[j, 0, 0:1, 128 * i : 128 * i + 1].astype(single) for i in range(3)]
            squares.append(parts[0] + parts[1] + parts[2])
    while len(squares) > 1:
        squares = [squares[i] + squares[i + 1] for i in range(0, len(squares), 2)]
    norm = jnp.sqrt(squares[0] + scalars[0])
    factor = clip_limit / jnp.maximum(norm, clip_limit)

    @pl.when(pl.program_id(0) == 0)
    def _():
        norm_out[...] = jnp.broadcast_to(norm, norm_out.shape)
        held = [item[...] for item in latents]
        fresh = adamw(*held, latent_grad[...] * factor[None], scalars[1], scalars[2])
        for target, item in zip(new_latents, fresh):
            target[...] = item

    for i in range(n_src):
        for j in range(per):
            at = pl.multiple_of(((i * per + j) ^ me[0]) * rows, rows)
            for h in range(3):
                grads[h, pl.ds(at, rows), :] = routed[i][j, h].astype(single)
    sort = kind[pl.program_id(0)]
    for h in range(3):
        thin = lax.dot_general(
            slot_out[0, h], slot_in[0], (((0,), (0,)), ((), ())), preferred_element_type=single
        )
        grad = jnp.where(sort == 1, grads[h], thin) * factor
        w, m, v = weight[0, h], moment[0, h], square[0, h]
        fresh_w, fresh_m, fresh_v = adamw(w, m, v, grad, scalars[1], scalars[2])
        new_weight[0, h] = jnp.where(sort == 0, w, fresh_w)
        new_moment[0, h] = jnp.where(sort == 0, m, fresh_m)
        new_square[0, h] = jnp.where(sort == 0, v, fresh_v)


def adam_places(me, kind, scalars, routed, slot_out, slot_in, held, latent_grad, latents):
    slots, width, depth = held[0].shape
    head = width // 3
    clips = slot_in.shape[1]
    rows = routed[0].shape[1]
    routed = [item.reshape((-1, 3 * slots + 1, rows, depth)) for item in routed]
    per = routed[0].shape[0]
    big = pl.BlockSpec((1, 3, head, depth), lambda s, *_: (s, 0, 0, 0))
    latents_shape = (latent_grad.shape[1], 2, depth)
    small = pl.BlockSpec(latents_shape, lambda s, *_: (0, 0, 0))
    out = pl.pallas_call(
        functools.partial(adam_kernel, len(routed)),
        out_shape=[jax.ShapeDtypeStruct((slots, 3, head, depth), single)] * 3
        + [jax.ShapeDtypeStruct(latents_shape, single) for _ in latents]
        + [jax.ShapeDtypeStruct((8, 128), single)],
        grid_spec=pltpu.PrefetchScalarGridSpec(
            num_scalar_prefetch=3,
            grid=(slots,),
            in_specs=[pl.BlockSpec((per, 3, rows, depth), lambda s, *_: (0, s, 0, 0))]
            * len(routed)
            + [pl.BlockSpec((per, 1, rows, depth), lambda s, *_: (0, 3 * slots, 0, 0))]
            * len(routed)
            + [
                pl.BlockSpec((1, 3, clips, head), lambda s, *_: (s, 0, 0, 0)),
                pl.BlockSpec((1, clips, depth), lambda s, *_: (s, 0, 0)),
                big,
                big,
                big,
            ]
            + [small] * 4,
            out_specs=[big] * 3 + [small] * 3 + [pl.BlockSpec((8, 128), lambda s, *_: (0, 0))],
            scratch_shapes=[pltpu.VMEM((3, head, depth), single)],
        ),
        compiler_params=pltpu.CompilerParams(vmem_limit_bytes=60 << 20),
    )(
        me,
        kind,
        scalars,
        *routed,
        *routed,
        slot_out.reshape(slots, clips, 3, head).swapaxes(1, 2),
        slot_in,
        *(item.reshape(slots, 3, head, depth) for item in held),
        latent_grad.swapaxes(0, 1),
        *(item.swapaxes(0, 1) for item in latents),
    )
    places = [item.reshape(slots, width, depth) for item in out[:3]]
    return places + [item.swapaxes(0, 1) for item in out[3:6]] + [out[6][0, 0]]


def normed(values):
    center = values - jnp.mean(values, axis=-1, keepdims=True)
    spread_sq = jnp.mean(center * center, axis=-1, keepdims=True)
    return center * lax.rsqrt(spread_sq + norm_epsilon)


def modulate(values, shift, scale):
    return normed(values) * (1.0 + scale[None, :]) + shift[None, :]


def modulate_back(values, shift, scale, grad):
    _, pullback = jax.vjp(modulate, values, shift, scale)
    return pullback(grad)


def sinusoid(timestep):
    half_width = D // 2
    frequency = jnp.exp(-math.log(10000.0) * jnp.arange(half_width).astype(single) / half_width)
    angles = timestep.astype(single)[:, None] * frequency[None, :]
    return jnp.concatenate([jnp.cos(angles), jnp.sin(angles)], axis=1)


def matmul(form, left, right):
    return jnp.einsum(form, left, right, preferred_element_type=single)


NT_DIMS = (((1,), (1,)), ((), ()))
TN_DIMS = (((0,), (0,)), ((), ()))


def dot(left, right, dims=(((1,), (0,)), ((), ()))):
    return lax.dot_general(left, right, dims, preferred_element_type=single)


def scores_of(keys, query, length):
    scores = dot(keys, query, NT_DIMS) * HD ** (-0.5)
    if length is None:
        return scores
    row = lax.broadcasted_iota(jnp.int32, scores.shape, 0)
    return jnp.where(row < length, scores, masked_score)


def attend_kernel(masked, length, query, keys, values, output, totals):
    limit = length[0] if masked else None
    rows = []
    for h in range(2):
        at = slice(h * HD, (h + 1) * HD)
        scores = scores_of(keys[:, at], query[:, at], limit)
        top = jnp.max(scores, axis=0, keepdims=True)
        shifted = jnp.exp(scores - top)
        total = jnp.sum(shifted, axis=0, keepdims=True)
        probs = (shifted * (1.0 / total)).astype(bfloat)
        rows.append(dot(values[:, at], probs, TN_DIMS))
        totals[0, h : h + 1, :] = top + jnp.log(total)
    output[...] = jnp.concatenate(rows, axis=0).T.astype(bfloat)


def attend_back_kernel(masked, length, query, keys, values, grad_out, totals, dq, dk, dv):
    limit = length[0] if masked else None
    query_rows, key_cols, value_cols = [], [], []
    for h in range(2):
        at = slice(h * HD, (h + 1) * HD)
        q, k, v, do = query[:, at], keys[:, at], values[:, at], grad_out[:, at]
        probs = jnp.exp(scores_of(k, q, limit) - totals[0, h : h + 1, :])
        grad_probs = dot(v, do, NT_DIMS)
        inner = jnp.sum(probs * grad_probs, axis=0, keepdims=True)
        grad_scores = (probs * (grad_probs - inner)).astype(bfloat)
        query_rows.append(dot(k, grad_scores, TN_DIMS))
        key_cols.append(dot(grad_scores, q))
        value_cols.append(dot(probs.astype(bfloat), do))
    scale = HD ** (-0.5)
    dq[...] = (jnp.concatenate(query_rows, axis=0).T * scale).astype(bfloat)
    dk[...] = (jnp.concatenate(key_cols, axis=1) * scale).astype(bfloat)
    dv[...] = jnp.concatenate(value_cols, axis=1).astype(bfloat)


def pair_call(kernel, length, ins, outs, flops):
    def spec(shape):
        if len(shape) == 3:
            return pl.BlockSpec((1,) + shape[1:], lambda i, *_: (i, 0, 0))
        return pl.BlockSpec((shape[0], 2 * HD), lambda i, *_: (0, i))

    masked = length is not None
    length = jnp.zeros((1,), jnp.int32) if length is None else length.reshape(1)
    return pl.pallas_call(
        functools.partial(kernel, masked),
        out_shape=outs,
        grid_spec=pltpu.PrefetchScalarGridSpec(
            num_scalar_prefetch=1,
            grid=(ins[0].shape[1] // (2 * HD),),
            in_specs=[spec(item.shape) for item in ins],
            out_specs=[spec(item.shape) for item in outs],
        ),
        compiler_params=pltpu.CompilerParams(vmem_limit_bytes=48 << 20),
        cost_estimate=pl.CostEstimate(
            flops=flops, bytes_accessed=8 << 20, transcendentals=6 * FRAMES * FRAMES
        ),
    )(length, *ins)


def attention(query, keys, values, length):
    shape = query.shape
    outs = [
        jax.ShapeDtypeStruct(shape, bfloat),
        jax.ShapeDtypeStruct((shape[1] // (2 * HD), 2, shape[0]), single),
    ]
    flops = 16 * shape[0] * keys.shape[0] * shape[1]
    return pair_call(attend_kernel, length, (query, keys, values), outs, flops)


def attention_back(query, keys, values, length, grad_out, totals):
    outs = [jax.ShapeDtypeStruct(item.shape, bfloat) for item in (query, keys, values)]
    flops = 40 * query.shape[0] * keys.shape[0] * query.shape[1]
    ins = (query, keys, values, grad_out, totals)
    return pair_call(attend_back_kernel, length, ins, outs, flops)


def spread(values):
    return jnp.concatenate([values, swap(values, "mc")], axis=0)


def collect(left, right):
    own = left.shape[0] // 2
    other = matmul("fk,kd->fd", left[own:], right).astype(bfloat)
    got = swap(other, "mc")
    return matmul("fk,kd->fd", left[:own], right) + got.astype(single)


def body(
    clean_latent,
    noise_draw,
    captions,
    caption_len,
    timestep,
    step_weight,
    step_count,
    unit_slot,
    master,
    first_moment,
    second_moment,
    latent_master,
    latent_first,
    latent_second,
):
    slots = master.shape[0]
    width = master.shape[1]
    n_dp = lax.axis_size("dp")
    index = lax.axis_index("dp")
    column = 2 * lax.axis_index("mx") + lax.axis_index("mc")
    clip = lax.axis_index("mx")
    clips = captions.shape[0]
    owner = unit_slot // slots
    place = unit_slot % slots
    local_ids = index * slots + jnp.arange(slots)
    pick = unit_slot[None, :] == local_ids[:, None]
    live_slot = jnp.any(pick, axis=1)

    table = jnp.arange(step_weight.shape[0])
    clip_weight = jnp.sum(
        jnp.where(timestep[:, None] == table[None, :], step_weight[None, :], 0.0), axis=1
    )
    cap_mask = jnp.arange(captions.shape[1])[None, :] < caption_len[:, None]
    pooled = (
        jnp.sum(jnp.where(cap_mask[:, :, None], captions.astype(single), 0.0), axis=1)
        / caption_len.astype(single)[:, None]
    )
    packed = jnp.concatenate(
        [sinusoid(timestep), pooled, jnp.broadcast_to(clip_weight[:, None], (clips, 128))], axis=1
    )

    master_low = master.astype(bfloat)
    split = master_low.reshape(slots, 3, n_dp, width // (3 * n_dp), D)
    blocks = [
        lax.dynamic_index_in_dim(split, index ^ k, 2, keepdims=False) for k in range(n_dp)
    ]
    def gather_packed():
        values = packed
        for i, bit in enumerate(reversed(range(dp_bits()))):
            values = jnp.stack([values, swap(values, "dp", bit)], axis=i)
        return values.reshape(n_dp * clips, -1)

    got, packed = exchange_dp(blocks, gather_packed)

    sinus_low = packed[:, :D].astype(bfloat)
    pooled_low = packed[:, D : 2 * D].astype(bfloat)
    weight_total = jnp.sum(packed[:, 2 * D])

    def held(u):
        return lax.dynamic_index_in_dim(master_low, place[u], 0, keepdims=False)

    zero = jnp.zeros((), bfloat)
    cond_part = matmul(
        "bd,ed->be", jnp.where(owner[24] == index, sinus_low, zero), held(24)
    ) + matmul("bd,ed->be", jnp.where(owner[25] == index, pooled_low, zero), held(25))
    row = jnp.arange(n_dp * clips)
    reorder = (row[:, None] ^ (index * clips)) == row[None, :]
    reorder = reorder.astype(single)

    def reordered(values):
        return jnp.einsum("bc,cd->bd", reorder, values, precision=highest)

    cond_part = pair(reordered(cond_part), 1, "mx")
    cond_part, *got = tie(cond_part, *got)
    unit_of = jnp.sum(
        jnp.where(
            unit_slot[None, :] == jnp.arange(n_dp * slots)[:, None],
            jnp.arange(UNITS)[None, :] + 1,
            0,
        ),
        axis=1,
    ) - 1
    table = jnp.stack(
        [
            unit_of.reshape(n_dp, slots)[jnp.array([d ^ k for k in range(n_dp)])]
            for d in range(n_dp)
        ]
    )
    unit_at = lax.dynamic_index_in_dim(table, index, 0, keepdims=False).reshape(-1)
    chunk_near, chunk_cross, chunk_up, chunk_down = place_blocks(got, unit_at, (4, 4, 4, 4))
    unit_tail = chunk_near.shape[1:]
    chunk_near, chunk_up, chunk_down, cond_part = tie(
        chunk_near, chunk_up, chunk_down, cond_part
    )
    near, cross = Gather(chunk_near), Gather(chunk_cross)
    near.send_ring()
    got_up, got_down = swap(chunk_up, "dp", 0), swap(chunk_down, "mx")
    cond_part = pair(cond_part, 2, "mc").reshape(n_dp * clips, D)
    for bit in range(dp_bits()):
        cond_part = cond_part + swap(cond_part, "dp", bit)
        if bit < 3:
            cond_part = land(cond_part, near)
            if bit < 2:
                near.send_ring()
        if bit == 1:
            cond_part, got_up, got_down = tie(cond_part, got_up, got_down)
    far = Gather(jnp.stack([chunk_up, got_up, chunk_down, got_down]).reshape((2, 2, 4) + unit_tail))
    cond = tie(reordered(cond_part))[0]
    active = jax.nn.silu(cond).astype(bfloat)
    all_rows = matmul("bd,sed->bse", active, master_low)
    ada = pick[:, 16:24]
    rows = jnp.einsum("sj,bse->bje", ada.astype(single), all_rows, precision=highest)
    rows = rows.reshape(n_dp, clips, 8, width)
    near_a, near_b = near.parts(2)
    rows, near_a.pieces, near_b.pieces, cross.ring[0] = tie(
        rows, near_a.pieces, near_b.pieces, cross.ring[0]
    )
    near_a.send(0)
    near_b.send("x")
    cross.send_ring()
    for bit in reversed(range(1, dp_bits())):
        half = rows.shape[0] // 2
        rows = rows[:half] + swap(rows[half:], "dp", bit)
        if bit == 2:
            rows = land(rows, near_a, near_b, cross)
            near_a.send("x")
            near_b.send(0)
            cross.send_ring()
    rows = land(rows, cross)
    rows, far.ring[0] = tie(rows, far.ring[0])
    cross.send_ring()
    far.send_ring()
    mine = lax.dynamic_index_in_dim(rows, clip, 1, keepdims=False)
    theirs = swap(lax.dynamic_index_in_dim(rows, 1 - clip, 1, keepdims=False), "mx")
    rows = jnp.stack(
        [jnp.where(clip == 0, mine, theirs), jnp.where(clip == 0, theirs, mine)], axis=2
    )
    rows = land(rows, near_a, near_b, cross)
    rows = rows[0] + swap(rows[1], "dp", 0)
    cross_a, cross_b = cross.parts(2)
    rows, cross_a.pieces, cross_b.pieces = tie(rows, cross_a.pieces, cross_b.pieces)
    rows = land(rows, far)
    cross_a.send(0)
    cross_b.send("x")
    far.send_ring()
    modulation = tie(pair(rows, 2, "mc").reshape(8, D))[0]

    text = lax.dynamic_index_in_dim(captions, clip, 0, keepdims=False)
    text_len = lax.dynamic_index_in_dim(caption_len, clip, 0, keepdims=False)
    my_step = lax.dynamic_index_in_dim(timestep, clip, 0, keepdims=False)
    my_weight = lax.dynamic_index_in_dim(clip_weight, clip, 0, keepdims=False)
    latents = jnp.stack([clean_latent, noise_draw], axis=1)
    away = swap(lax.dynamic_index_in_dim(latents, 1 - clip, 0, keepdims=False), "mx")
    latents = jnp.concatenate(
        [lax.dynamic_index_in_dim(latents, clip, 0, keepdims=False), away], axis=1
    )
    level = (my_step.astype(single) + 0.5) / NT
    noisy = (1.0 - level) * latents[0] + level * latents[1]
    target = latents[1] - latents[0]

    hidden_zero = jnp.einsum("fc,cd->fd", noisy, latent_master[0], precision=highest)
    first_in = spread(modulate(hidden_zero, modulation[0], modulation[1]).astype(bfloat))
    first_in = land(first_in, cross_a, cross_b, far)
    cross_a.send("x")
    cross_b.send(0)
    far.send_ring()
    w_self = jnp.concatenate([near_a.laid(), near_b.laid()], axis=0)
    self_query, self_keys, self_values = (
        matmul("fd,ed->fe", first_in, w_self[u]).astype(bfloat) for u in range(3)
    )
    self_query = land(self_query, cross_a, cross_b, far)
    up, down = far.parts(2)
    up.pieces, down.pieces = tie(up.pieces[:, 0], down.pieces[:, 0])
    up.send("x")
    down.send(0)
    self_flat, self_total = attention(self_query, self_keys, self_values, None)
    self_branch = collect(self_flat, w_self[3])
    hidden_one = hidden_zero + modulation[2] * self_branch
    second_in = spread(normed(hidden_one).astype(bfloat))
    w_cross = jnp.concatenate([cross_a.laid(), cross_b.laid()], axis=0)
    weights = [w_self[i] for i in range(4)] + [w_cross[i] for i in range(4)]
    cross_query = matmul("fd,ed->fe", second_in, weights[4]).astype(bfloat)
    cross_query, got_up, got_down = tie(cross_query, up.got, down.got)
    cross_keys = matmul("ld,ed->le", text, weights[5]).astype(bfloat)
    cross_values = matmul("ld,ed->le", text, weights[6]).astype(bfloat)
    cross_flat, cross_total = attention(cross_query, cross_keys, cross_values, text_len)
    cross_branch = collect(cross_flat, weights[7])
    hidden_two = hidden_one + cross_branch
    third_in = spread(modulate(hidden_two, modulation[3], modulation[4]).astype(bfloat))
    w_up = jnp.stack([up.pieces, got_up], axis=1).reshape(-1, D)
    w_down = jnp.stack([down.pieces, got_down], axis=2).reshape(-1, D)
    upper = matmul("fd,kd->fk", third_in, w_up).astype(bfloat)
    upper_wide = upper.astype(single)
    activated = jax.nn.gelu(upper_wide, approximate=True).astype(bfloat)
    mlp_branch = collect(activated, w_down)
    hidden_three = hidden_two + modulation[5] * mlp_branch
    final_wide = modulate(hidden_three, modulation[6], modulation[7]).astype(bfloat).astype(single)
    predicted = jnp.einsum("fd,cd->fc", final_wide, latent_master[1], precision=highest)
    error = predicted - target
    loss_local = jnp.sum(my_weight * error * error)

    grad_pred = 2.0 / (C * FRAMES) * my_weight * error / weight_total
    grad_out_proj = jnp.einsum("fc,fd->cd", grad_pred, final_wide, precision=highest)
    grad_final = jnp.einsum("fc,cd->fd", grad_pred, latent_master[1], precision=highest)
    grad_three, shift_f, scale_f = modulate_back(
        hidden_three, modulation[6], modulation[7], grad_final
    )
    gate_m_grad = jnp.sum(grad_three * mlp_branch, axis=0)
    grad_mlp = spread((modulation[5] * grad_three).astype(bfloat))
    grad_w_down = matmul("fk,fd->kd", activated, grad_mlp)
    down = Scatter(cut_far(grad_w_down, unit_tail, True))
    grad_mlp, down.pieces = tie(grad_mlp, down.pieces)
    down.send("x")
    grad_act = matmul("fd,kd->fk", grad_mlp, w_down)
    _, gelu_back = jax.vjp(lambda inner_in: jax.nn.gelu(inner_in, approximate=True), upper_wide)
    grad_upper = gelu_back(grad_act)[0].astype(bfloat)
    grad_w_up = matmul("fk,fd->kd", grad_upper, third_in)
    up = Scatter(cut_far(grad_w_up, unit_tail, False))
    up.send(0)
    grad_third = collect(grad_upper, w_up)
    grad_two, shift_m, scale_m = modulate_back(hidden_two, modulation[3], modulation[4], grad_third)
    grad_two = grad_two + grad_three
    grad_cross = spread(grad_two.astype(bfloat))
    grad_cross_flat = matmul("fd,kd->fk", grad_cross, weights[7]).astype(bfloat)
    grad_w_cross_out = matmul("fk,fd->kd", cross_flat, grad_cross)
    cq_grad, ck_grad, cv_grad = attention_back(
        cross_query, cross_keys, cross_values, text_len, grad_cross_flat, cross_total
    )
    cq_grad = land(cq_grad, down, up)
    down.send(0)
    up.send("x")
    grad_w_cq = matmul("fk,fd->kd", cq_grad, second_in)
    grad_w_ck = matmul("lk,ld->kd", ck_grad, text)
    grad_w_cv = matmul("lk,ld->kd", cv_grad, text)
    cross_a = Scatter(cut_units(jnp.stack([grad_w_cq, grad_w_ck]), True))
    cross_b = Scatter(cut_units(jnp.stack([grad_w_cv, grad_w_cross_out]), False))
    cross_a.send("x")
    cross_b.send(0)
    grad_second = collect(cq_grad, weights[4])
    _, norm_back = jax.vjp(normed, hidden_one)
    grad_one = grad_two + norm_back(grad_second)[0]
    gate_a_grad = jnp.sum(grad_one * self_branch, axis=0)
    grad_self = spread((modulation[2] * grad_one).astype(bfloat))
    grad_self_flat = matmul("fd,kd->fk", grad_self, weights[3]).astype(bfloat)
    grad_self_flat = land(grad_self_flat, down, up)
    far = up.join(down)
    far.send_ring()
    grad_w_self_out = matmul("fk,fd->kd", self_flat, grad_self)
    self_grads = attention_back(
        self_query, self_keys, self_values, None, grad_self_flat, self_total
    )
    self_grads = jnp.concatenate(self_grads, axis=1)
    self_grads = land(self_grads, cross_a, cross_b, far)
    far.send_ring()
    cross_a.send(0)
    cross_b.send("x")
    grad_w_attn = matmul("fk,fd->kd", self_grads, first_in)
    grad_w_attn = land(grad_w_attn, far)
    far.send_ring()
    near_a = Scatter(cut_units(grad_w_attn[: 4 * width].reshape(2, 2 * width, D), True))
    near_b = Scatter(cut_units(jnp.stack([grad_w_attn[4 * width :], grad_w_self_out]), False))
    near_a.send("x")
    near_b.send(0)
    grad_first = collect(self_grads, jnp.concatenate(weights[0:3], axis=0))
    grad_first = land(grad_first, cross_a, cross_b)
    cross = cross_a.join(cross_b)
    cross.send_ring()
    grad_zero, shift_a, scale_a = modulate_back(
        hidden_zero, modulation[0], modulation[1], grad_first
    )
    grad_zero = land(grad_zero, near_a, near_b, cross, far)
    cross.send_ring()
    near_a.send(0)
    near_b.send("x")
    grad_zero = grad_zero + grad_one
    grad_in_proj = jnp.einsum("fc,fd->cd", noisy, grad_zero, precision=highest)

    grad_mod = jnp.stack(
        [shift_a, scale_a, gate_a_grad, shift_m, scale_m, gate_m_grad, shift_f, scale_f], axis=0
    )
    grad_mod = (grad_mod + swap(grad_mod, "mc")).astype(bfloat)
    for i, bit in enumerate(reversed(range(1, dp_bits()))):
        grad_mod = jnp.stack([grad_mod, swap(grad_mod, "dp", bit)], axis=i)
        if i == 0:
            grad_mod = land(grad_mod, near_a, near_b, cross)
            near = near_a.join(near_b).pieces
            z_got = [shift(near[j], -j) for j in range(1, high())]
            cross.send_ring()
    grad_mod = pair(grad_mod, dp_bits() - 1, "mx")
    grad_mod = jnp.stack([grad_mod, swap(grad_mod, "dp", 0)], axis=dp_bits() - 1)
    grad_mod = tie(grad_mod.reshape(n_dp * clips, 8, D))[0]
    mod_cols = lax.dynamic_index_in_dim(
        grad_mod.reshape(n_dp * clips, 8, D // width, width), column, 2, keepdims=False
    )
    slot_mod = matmul("sj,bje->sbe", ada.astype(bfloat), mod_cols).astype(bfloat)
    grad_active = matmul("sbe,sed->bd", slot_mod, master_low)
    small = jnp.concatenate([grad_in_proj, grad_out_proj], axis=0)
    pad = jnp.full((2 * C, 128), loss_local, single)
    mixed = jnp.concatenate(
        [
            jnp.pad(reordered(grad_active), ((0, 0), (0, 128))),
            jnp.concatenate([small, pad], axis=1),
        ],
        axis=0,
    )
    mixed = sum_mp(mixed)
    total = near[0].astype(single)
    for item in z_got:
        total = total + item.astype(single)
    cross.take(cross.got)
    reduced = [total] + [item.sum.astype(single) for item in (cross, far)]
    reduced = jnp.concatenate(reduced, axis=0)
    wide_square = sum_mp(jnp.broadcast_to(jnp.sum(reduced * reduced), (8, 128)))
    wide_at = jnp.where((unit_at >= 0) & (unit_at < WIDE), unit_at, 0)
    wide_square, mixed = tie(wide_square, mixed)
    mixed = sum_dp(mixed)
    grad_active, small = reordered(mixed[: n_dp * clips, :D]), mixed[n_dp * clips :]
    latent_grad = small[:, :D].reshape(2, C, D)
    loss_sum = small[0, D]
    routes = route_blocks(reduced.astype(bfloat), wide_at, wide_square, n_dp)
    routed = exchange_dp(routes)
    _, silu_back = jax.vjp(jax.nn.silu, cond)
    grad_cond = silu_back(grad_active)[0].astype(bfloat)
    cond_cols = lax.dynamic_index_in_dim(
        grad_cond.reshape(n_dp * clips, D // width, width), column, 1, keepdims=False
    )
    is_time, is_pool = pick[:, 24], pick[:, 25]
    slot_out = jnp.where((is_time | is_pool)[:, None, None], cond_cols[None], slot_mod)
    slot_in = jnp.where(
        is_time[:, None, None],
        sinus_low[None],
        jnp.where(is_pool[:, None, None], pooled_low[None], active[None]),
    )
    def gram(values):
        return matmul("bd,cd->bc", values, values)

    flat_mod = grad_mod.reshape(n_dp * clips, 8 * D)
    thin_square = jnp.sum(gram(active) * gram(flat_mod)) + jnp.sum(
        (gram(sinus_low) + gram(pooled_low)) * gram(grad_cond)
    )

    rest_square = thin_square + jnp.sum(latent_grad * latent_grad)
    count = step_count[0].astype(single)
    is_wide = jnp.any(pick[:, :WIDE], axis=1)
    kind = jnp.where(is_wide, 1, jnp.where(live_slot, 2, 0)).astype(jnp.int32)
    fixes = [1.0 / (1.0 - jnp.power(beta, count)) for beta in (beta_first, beta_second)]
    *outputs, grad_norm = adam_places(
        index.reshape(1).astype(jnp.int32),
        kind,
        jnp.stack([rest_square] + fixes),
        routed,
        slot_out,
        slot_in,
        (master, first_moment, second_moment),
        latent_grad,
        (latent_master, latent_first, latent_second),
    )
    loss_value = loss_sum / (C * FRAMES * weight_total)
    return (*outputs, grad_norm, loss_value)


def solution(mesh):
    n_dp, n_mp = mesh.shape["dp"], mesh.shape["mp"]
    fine = Mesh(mesh.devices.reshape(n_dp, n_mp // 2, 2), ("dp", "mx", "mc"))
    frames = P("dp", ("mx", "mc"), None)
    placed = (
        frames,
        frames,
        P("dp", None, None),
        P("dp"),
        P("dp"),
        P(),
        P(),
        P(),
        frames,
        frames,
        frames,
        P(),
        P(),
        P(),
    )
    return jax.shard_map(
        body,
        mesh=fine,
        in_specs=placed,
        out_specs=(frames, frames, frames, P(), P(), P(), P(), P()),
        check_vma=False,
    )
```
